512 devices in a mesh: section: 4 (over y), dp: 32 (over x, z_lo), tensor: 4 (over z_hi, core).
Axes of the slice: x: 4, y: 4, z: 16 (z_hi: 2, z_lo: 8; z = z_hi * 8 + z_lo), core: 2. Of those that a mesh axis runs over, the one named last changes fastest.
Arguments:
- stored_copies: bfloat16 [4, 2, 4096, 9216], P('section', None, 'dp', 'tensor'), may hold values from -80 to 80, as said below
- entry_codes: bfloat16 [4096, 9216], P('dp', 'tensor'), may hold values from -1 to 1
- exit_grad_codes: bfloat16 [4096, 9216], P('dp', 'tensor'), may hold values from -1 to 1
- exit_grad_scales: float32 [4096], P('dp'), may hold values from 0 to 0.28125, as said below
- slot_ids: int32 [32, 4], P('dp'), may hold values from 0 to 3, each once within a row
- norm_gain: float32 [4, 9216], P('section', 'tensor'), may hold values from 0.1 to 1.9
- down_proj: bfloat16 [4, 384, 9216], P('section', 'dp', 'tensor'), may hold values from -0.0625 to 0.0625
- up_proj: bfloat16 [4, 384, 9216], P('section', 'dp', 'tensor'), may hold values from -0.3125 to 0.3125
Outputs:
- sent_codes: bfloat16 [4, 4096, 9216], P('section', 'dp', 'tensor')
- returned_codes: bfloat16 [4, 4096, 9216], P('section', 'dp', 'tensor')
- grad_down: float32 [4, 384, 9216], P('section', 'dp', 'tensor')
- grad_up: float32 [4, 384, 9216], P('section', 'dp', 'tensor')
The draws below stay inside these ranges and needn't reach their ends.
Inputs may be any that keep to these rules, and one draw needn't show every extreme that they name: `stored_copies`: the output copy of each section but the last equals the input copy of the next section. `exit_grad_scales`: Positive. `slot_ids`: each row holds every slot number once.
All inputs are finite; a program needn't handle non-finite values. Where the reference program divides by a largest or mean magnitude, that divisor is 1e-20 or more.
Results may differ from the reference program's by a relative error of at most 0.033.
Values may be sent and summed in bfloat16 or wider, within the bound.
A program may use at most 64 MiB of HBM per device.

```python
import math
import jax
import jax.numpy as jnp
from jax import lax

D = 9216
BOT = 384
MICRO = 4
ROWS = 32
TOKENS = 4096
N_SECTION = 4
N_DP = 32


def draw_stored_copies(key, part):
    key = jax.random.fold_in(key, 11)
    value_key, scale_key, offset_key, sign_key = jax.random.split(key, 4)
    row_count = N_DP * MICRO * ROWS
    offset_level = jax.random.uniform(offset_key, (N_SECTION + 1, row_count, 1), jnp.float32, 0.5, 1.5)
    offset_sign = jnp.where(jax.random.bernoulli(sign_key, 0.5, (N_SECTION + 1, row_count, 1)), 1.0, -1.0)
    values = jnp.clip(jax.random.normal(value_key, (N_SECTION + 1, row_count, D), jnp.float32), -4.0, 4.0)
    row_scale = jnp.exp(jax.random.uniform(scale_key, (N_SECTION + 1, row_count, 1), jnp.float32, math.log(0.25), math.log(4.0)))
    rising = 1.0 + 2.0 * jnp.arange(D, dtype=jnp.float32) / D
    copy_bank = ((values + offset_sign * offset_level) * row_scale * rising).astype(jnp.bfloat16)
    return jnp.stack([copy_bank[:-1], copy_bank[1:]], axis=1)


def draw_exit_grad_scales(key, part):
    key = jax.random.fold_in(key, 23)
    position = jnp.arange(TOKENS, dtype=jnp.float32) / TOKENS
    base_scale = jnp.exp(jax.random.uniform(key, (TOKENS,), jnp.float32, math.log(0.3), math.log(3.0)))
    rising_ramp = 1.0 + 2.0 * position
    return base_scale * rising_ramp / math.sqrt(TOKENS)


def steps_of(key, dims, cuts, smallest, top_value):
    level = 1.0
    for dim, parts in cuts:
        steps = jax.random.uniform(jax.random.fold_in(jax.random.fold_in(key, 6), dim), (parts,), jnp.float32, smallest / len(cuts), top_value / len(cuts))
        level = level * jnp.repeat(jnp.exp(steps), dims[dim] // parts).reshape((-1,) + (1,) * (len(dims) - 1 - dim))
    return level


def gaussian(rng, shape, width, limit, cuts=(), held_as=jnp.bfloat16):
    values = width * jax.random.normal(rng, shape, jnp.float32)
    if cuts:
        values = values * steps_of(rng, shape, cuts, -0.22, 0.18)
    return jnp.clip(values, -limit, limit).astype(held_as)


def setup_inputs(seed: int = 0) -> dict:
    key_of = jax.random.split(jax.random.key(seed), 9)
    return {
        "stored_copies": draw_stored_copies(jax.random.fold_in(key_of[8], 71), 0),
        "entry_codes": jnp.clip(jax.random.uniform(key_of[1], (TOKENS, D), jnp.float32, -1.0, 1.0) * steps_of(key_of[1], (TOKENS, D), ((0, 32), (1, 4)), -0.4, 0.0), -1.0, 1.0).astype(jnp.bfloat16),
        "exit_grad_codes": jnp.clip(jax.random.uniform(key_of[2], (TOKENS, D), jnp.float32, -1.0, 1.0) * steps_of(key_of[2], (TOKENS, D), ((0, 32), (1, 4)), -0.4, 0.0), -1.0, 1.0).astype(jnp.bfloat16),
        "exit_grad_scales": draw_exit_grad_scales(jax.random.fold_in(key_of[8], 71), 0),
        "slot_ids": jax.vmap(lambda own: jax.random.permutation(own, MICRO))(jax.random.split(key_of[4], N_DP)).reshape((N_DP, MICRO)).astype(jnp.int32),
        "norm_gain": jnp.clip(1.0 + 0.18 * jax.random.normal(key_of[5], (N_SECTION, D), jnp.float32), 0.1, 1.9),
        "down_proj": gaussian(key_of[6], (N_SECTION, BOT, D), D ** -0.5, 0.0625, ((0, 4), (1, 32), (2, 4))),
        "up_proj": gaussian(key_of[7], (N_SECTION, BOT, D), BOT ** -0.5, 0.3125, ((0, 4), (1, 32), (2, 4))),
    }


def copy_rows(copy_bank, slot_ids):
    blocks = copy_bank.reshape(N_DP, MICRO, ROWS, D)
    chosen = jax.vmap(lambda block_rows, slot_order: jnp.take(block_rows, slot_order, axis=0))(blocks, slot_ids)
    return chosen.reshape(TOKENS, D).astype(jnp.float32)

def row_spread(copies):
    return 2.0 * jnp.sqrt(lax.optimization_barrier(jnp.mean(copies * copies, axis=1, keepdims=True)) + 1e-05)

def replica_sum(left_side, right_side):
    left_rows = left_side.astype(jnp.float32).reshape(N_DP, MICRO * ROWS, left_side.shape[1])
    right_rows = right_side.astype(jnp.float32).reshape(N_DP, MICRO * ROWS, right_side.shape[1])
    partial_terms = jnp.einsum('rtk,rtj->rkj', left_rows, right_rows)
    rounded = lax.optimization_barrier(partial_terms.astype(jnp.bfloat16))
    return lax.optimization_barrier(jnp.sum(rounded.astype(jnp.float32), axis=0))

def reference(stored_copies, entry_codes, exit_grad_codes, exit_grad_scales, slot_ids, norm_gain, down_proj, up_proj):
    stored_state = []
    sent_list = []
    incoming = entry_codes
    for section_index in range(N_SECTION):
        copy_in = copy_rows(stored_copies[section_index, 0], slot_ids)
        section_input = copy_in + row_spread(copy_in) * incoming.astype(jnp.float32)
        row_mean = lax.optimization_barrier(jnp.mean(section_input, axis=1, keepdims=True))
        centred = section_input - row_mean
        variance = lax.optimization_barrier(jnp.mean(centred * centred, axis=1, keepdims=True))
        inverse_scale = lax.rsqrt(variance + 1e-05)
        normed = centred * inverse_scale
        scaled = (normed * norm_gain[section_index].astype(jnp.float32)).astype(jnp.bfloat16)
        inner_rows = jnp.dot(scaled, down_proj[section_index].T, preferred_element_type=jnp.float32)
        hidden = jax.nn.gelu(inner_rows).astype(jnp.bfloat16)
        result = section_input + jnp.dot(hidden, up_proj[section_index], preferred_element_type=jnp.float32)
        copy_out = copy_rows(stored_copies[section_index, 1], slot_ids)
        codes_out = jnp.clip((result - copy_out) / row_spread(copy_out), -1.0, 1.0).astype(jnp.bfloat16)
        sent_list.append(codes_out)
        stored_state.append((normed, inverse_scale, scaled, inner_rows, hidden))
        incoming = codes_out
    upstream = exit_grad_codes.astype(jnp.float32) * exit_grad_scales[:, None]
    grads_down = [None] * N_SECTION
    grads_up = [None] * N_SECTION
    returned_list = [None] * N_SECTION
    for section_index in reversed(range(N_SECTION)):
        normed, inverse_scale, scaled, inner_rows, hidden = stored_state[section_index]
        upstream_half = upstream.astype(jnp.bfloat16)
        grads_up[section_index] = replica_sum(hidden, upstream_half)
        back_grad = jnp.dot(upstream_half, up_proj[section_index].T, preferred_element_type=jnp.float32)
        unused_value, pull_back = jax.vjp(jax.nn.gelu, inner_rows)
        grad_inner = pull_back(back_grad)[0].astype(jnp.bfloat16)
        grads_down[section_index] = replica_sum(grad_inner, scaled)
        grad_normed = jnp.dot(grad_inner, down_proj[section_index], preferred_element_type=jnp.float32) * norm_gain[section_index].astype(jnp.float32)
        mean_grad = lax.optimization_barrier(jnp.mean(grad_normed, axis=1, keepdims=True))
        mean_cross = lax.optimization_barrier(jnp.mean(grad_normed * normed, axis=1, keepdims=True))
        grad_input = upstream + inverse_scale * (grad_normed - mean_grad - normed * mean_cross)
        row_peak = (lax.optimization_barrier(jnp.max(jnp.abs(grad_input), axis=1, keepdims=True)) + 1e-05).astype(jnp.bfloat16)
        row_peak = lax.optimization_barrier(row_peak).astype(jnp.float32)
        codes_back = (grad_input / row_peak).astype(jnp.bfloat16)
        returned_list[section_index] = codes_back
        upstream = codes_back.astype(jnp.float32) * row_peak
    return (jnp.stack(sent_list), jnp.stack(returned_list), jnp.stack(grads_down), jnp.stack(grads_up))
```

```python
import math

import jax
import jax.numpy as jnp
from jax import lax
from jax.experimental import pallas as pl
from jax.experimental.pallas import tpu as pltpu
from jax.sharding import PartitionSpec as P

MESH = pl.DeviceIdType.MESH
F32 = jnp.float32
BF16 = jnp.bfloat16
MICRO = 4
ROWS = 32
NX = 4
PAD = 16
DOWN, UP = 0, 1
CURVE = math.sqrt(2.0 / math.pi)


def by_rows(left, right):
    return lax.dot_general(left, right, (((1,), (1,)), ((), ())), preferred_element_type=F32)


def by_cols(left, right):
    return lax.dot_general(left, right, (((0,), (0,)), ((), ())), preferred_element_type=F32)


def times(left, right):
    return jnp.dot(left, right, preferred_element_type=F32)


def lane_mask(shift):
    row = lax.broadcasted_iota(jnp.int32, (ROWS, 128), 0)
    lane = lax.broadcasted_iota(jnp.int32, (ROWS, 128), 1)
    return lane == row + shift


def to_lanes(column, shift):
    return jnp.sum(jnp.where(lane_mask(shift), column, 0.0), 0, keepdims=True)


def to_column(lanes, shift):
    return jnp.sum(jnp.where(lane_mask(shift), lanes, 0.0), 1, keepdims=True)


def spread_matrix(shards, unit):
    shape = (shards * unit, shards * PAD)
    row = lax.broadcasted_iota(jnp.int32, shape, 0)
    col = lax.broadcasted_iota(jnp.int32, shape, 1)
    shard = jnp.zeros(shape, jnp.int32)
    for k in range(1, shards):
        shard += jnp.where(row >= k * unit, 1, 0)
    return jnp.where(col == shard * PAD + row - shard * unit, 1.0, 0.0)


def relay_kernel(
    nz, copies, entry, exit_codes, exit_scale, slots, gain_ref, shard,
    sent, returned, grad_down, grad_up,
    zbuf, wv, span_src, span_in, spans, incf, incb, xs, norm_stat, scaled, pres, hidden, gsum,
    p1s, p1r, t1s, t1r, p2s, p2r, t2s, t2r, u1s, u1r, u2s, u2r,
    gs, gb, dpre_s, dxb, peak_src, peak_in, gp, rx1, rx2, zs, rz,
    span_sem, zsend, zrecv, xsend, xrecv, l1send, l1recv, l2send, l2recv,
    b1send, b1recv, b2send, b2recv, ysend, yrecv, wsend, wrecv, peak_sem,
    gxsend, gxrecv, gzsend, gzrecv,
):
    sec = lax.axis_index("section")
    last = lax.axis_size("section") - 1
    dp = lax.axis_index("dp")
    ten = lax.axis_index("tensor")
    x = dp // nz
    z = dp % nz
    half_z = nz // 2
    unit = grad_down.shape[0]
    cols = gain_ref.shape[1]
    half = cols // 2
    bot = pres.shape[2]
    total = cols * 4
    xr, xl, xo = (x + 1) % NX, (x + NX - 1) % NX, (x + 2) % NX
    to_right = {"dp": xr * nz + z}
    to_left = {"dp": xl * nz + z}
    mate = {"tensor": ten + 1 - 2 * (ten % 2)}
    far = {"tensor": (ten + 2) % 4}
    others = [{"tensor": (ten + k) % 4} for k in (1, 2, 3)]
    next_sec = {"section": (sec + 1) % (last + 1)}
    prev_sec = {"section": (sec + last) % (last + 1)}
    z_up = {"dp": x * nz + (z + 1) % nz}
    z_down = {"dp": x * nz + (z + nz - 1) % nz}

    barrier = pltpu.get_barrier_semaphore()
    friends = others + [next_sec, prev_sec, to_right, to_left, z_up, z_down]
    for friend in friends:
        pl.semaphore_signal(barrier, inc=1, device_id=friend, device_id_type=MESH)
    pl.semaphore_wait(barrier, len(friends))

    def move(src, dst, send, recv, device):
        return pltpu.make_async_remote_copy(
            src_ref=src, dst_ref=dst, send_sem=send, recv_sem=recv,
            device_id=device, device_id_type=MESH,
        )

    def z_move(way, slot, m):
        return move(
            zbuf.at[slot, m], zbuf.at[slot, m], zsend.at[way, slot, m], zrecv.at[slot, m],
            z_up if way == 0 else z_down,
        )

    def z_step(k):
        for m in (DOWN, UP):
            @pl.when(z - k >= 0)
            def _():
                z_move(0, z - k, m).wait_recv()

                @pl.when(z < nz - 1)
                def _():
                    z_move(0, z - k, m).start()

            @pl.when(z + k < nz)
            def _():
                z_move(1, z + k, m).wait_recv()

                @pl.when(z > 0)
                def _():
                    z_move(1, z + k, m).start()

    def z_steps(first, end):
        def step(k, carry):
            z_step(k)
            return carry

        lax.fori_loop(first, end, step, 0)

    group = [z // half_z, 1 - z // half_z]

    def x_move(p, m, kind):
        g = group[p]
        block, device, part = {
            0: (x, to_right, slice(None)),
            1: (x, to_left, slice(None)),
            2: (xl, to_right, slice(0, half)),
            3: (xr, to_left, slice(half, cols)),
        }[kind]
        ref = wv.at[m, block, g] if kind < 2 else wv.at[m, block, g, :, part]
        return move(ref, ref, xsend.at[p, m, kind], xrecv.at[p, m, kind], device)

    def x_arrival(p, m, kind):
        g = group[p]
        ref = {
            0: lambda: wv.at[m, xl, g],
            1: lambda: wv.at[m, xr, g],
            2: lambda: wv.at[m, xo, g, :, slice(0, half)],
            3: lambda: wv.at[m, xo, g, :, slice(half, cols)],
        }[kind]()
        move(ref, ref, xsend.at[p, m, kind], xrecv.at[p, m, kind], to_right).wait_recv()

    def x_own(p, m):
        block = zbuf[pl.ds(group[p] * half_z, half_z), m].reshape(half_z * PAD, cols)
        pick = spread_matrix(half_z, unit).astype(BF16)
        wv[m, x, group[p]] = times(pick, block).astype(BF16)
        x_move(p, m, 0).start()
        x_move(p, m, 1).start()

    def x_forward(p, m):
        x_arrival(p, m, 0)
        x_move(p, m, 2).start()
        x_arrival(p, m, 1)
        x_move(p, m, 3).start()

    def x_finish(p, m):
        x_arrival(p, m, 2)
        x_arrival(p, m, 3)

    zbuf[z] = shard[...]

    for m in (DOWN, UP):
        @pl.when(z < nz - 1)
        def _():
            z_move(0, z, m).start()

        @pl.when(z > 0)
        def _():
            z_move(1, z, m).start()

    @pl.when(sec == 0)
    def _():
        incf[...] = entry[...]

    def squares(m, carry):
        sums = []
        for k in range(2):
            rows = copies[k, slots[m]].astype(F32)
            sums.append(to_lanes(jnp.sum(rows * rows, 1, keepdims=True), m * ROWS))
        return carry[0] + sums[0], carry[1] + sums[1]

    nothing = jnp.zeros((1, 128), F32)
    square_in, square_out = lax.fori_loop(0, MICRO, squares, (nothing, nothing))
    span_src[...] = jnp.zeros((8, 128), F32)
    span_src[0:1] = square_in
    span_src[1:2] = square_out

    def span_move(k):
        return move(span_src, span_in.at[k], span_sem.at[0, k], span_sem.at[1, k], others[k])

    for k in range(3):
        span_move(k).start()

    z_steps(1, half_z)
    for m in (DOWN, UP):
        x_own(0, m)
    z_steps(half_z, half_z + 2)
    x_forward(0, DOWN)
    z_steps(half_z + 2, half_z + 3)
    x_forward(0, UP)
    z_steps(half_z + 3, nz)
    for m in (DOWN, UP):
        x_own(1, m)
    for k in range(3):
        span_move(k).wait_recv()
    spans[...] = 2.0 * jnp.sqrt(
        (span_src[...] + span_in[0] + span_in[1] + span_in[2]) / total + 1e-05
    )
    for m in (DOWN, UP):
        x_forward(1, m)
    x_finish(0, DOWN)
    x_finish(1, DOWN)

    def weights(m):
        return wv[m].reshape(bot, cols)

    gain = gain_ref[...]
    first = gain.astype(BF16).astype(F32)
    second = (gain - first).astype(BF16).astype(F32)
    third = gain - first - second
    row = lax.broadcasted_iota(jnp.int32, (PAD, cols), 0)
    terms = jnp.where(
        row == 0, first, jnp.where(row == 1, second, jnp.where(row == 2, third, 0.0))
    ).astype(BF16)
    gain_down = jnp.sum(by_rows(terms, weights(DOWN)), 0, keepdims=True)
    pieces = bot // 128

    def put_stat(ref, m, mean, spread, gd):
        ref[m] = jnp.zeros((8, 128), F32)
        ref[m, 0:1] = to_lanes(mean, 0)
        ref[m, 1:2] = to_lanes(spread, 0)
        for i in range(pieces):
            ref[m, 2 + i : 3 + i] = gd[:, i * 128 : (i + 1) * 128]

    def get_stat(ref, m):
        gd = jnp.concatenate([ref[m, 2 + i : 3 + i] for i in range(pieces)], axis=1)
        return to_column(ref[m, 0:1], 0), to_column(ref[m, 1:2], 0), gd

    def join(count, p, mean, spread, gd, p_other, mean_other, spread_other, gd_other):
        both = 0.5 * (mean + mean_other)
        mine, theirs = mean - both, mean_other - both
        spread_both = spread + spread_other + count * (mine * mine + theirs * theirs)
        p_both = (p + p_other) + (mine * gd + theirs * gd_other)
        return p_both, both, spread_both, gd + gd_other

    def l1(m):
        return (
            move(p1s.at[m], p1r.at[m], l1send.at[m, 0], l1recv.at[m, 0], mate),
            move(t1s.at[m], t1r.at[m], l1send.at[m, 1], l1recv.at[m, 1], mate),
        )

    def l2(m):
        return (
            move(p2s.at[m], p2r.at[m], l2send.at[m, 0], l2recv.at[m, 0], far),
            move(t2s.at[m], t2r.at[m], l2send.at[m, 1], l2recv.at[m, 1], far),
        )

    def y_forward(m):
        return move(sent.at[m], incf.at[m], ysend.at[m], yrecv.at[m], next_sec)

    def y_back(m):
        return move(dxb.at[m], incb.at[m], wsend.at[m], wrecv.at[m], prev_sec)

    def forward_in(m):
        @pl.when(sec > 0)
        def _():
            y_forward(m).wait_recv()

        span = to_column(spans[0:1], m * ROWS)
        rows = copies[0, slots[m]].astype(F32) + span * incf[m].astype(F32)
        xs[m] = rows
        mean = jnp.sum(rows, 1, keepdims=True) / cols
        centred = rows - mean
        spread = jnp.sum(centred * centred, 1, keepdims=True)
        part = by_rows((centred * gain_ref[...]).astype(BF16), weights(DOWN))
        p1s[m] = part
        put_stat(t1s, m, mean, spread, gain_down)
        for copy in l1(m):
            copy.start()
        for copy in l1(m):
            copy.wait_recv()
        part, mean, spread, gd = join(
            float(cols), part, mean, spread, gain_down, p1r[m], *get_stat(t1r, m)
        )
        p2s[m] = part.astype(BF16)
        put_stat(t2s, m, mean, spread, gd)
        for copy in l2(m):
            copy.start()

    def forward_out(m):
        for copy in l2(m):
            copy.wait_recv()
        raw, mean, spread, gd = join(
            float(2 * cols), p2s[m].astype(F32), *get_stat(t2s, m),
            p2r[m].astype(F32), *get_stat(t2r, m)
        )
        inverse = lax.rsqrt(spread / total + 1e-05)
        pre = raw * inverse
        gsum[...] = gd
        pres[m] = pre
        norm_stat[m, 0] = mean
        norm_stat[m, 1] = inverse
        act = (0.5 * pre * (1.0 + jnp.tanh(CURVE * (pre + 0.044715 * (pre * pre * pre))))).astype(BF16)
        hidden[m] = act
        result = xs[m] + times(act, weights(UP))
        span = to_column(spans[1:2], m * ROWS)
        sent[m] = jnp.clip(
            (result - copies[1, slots[m]].astype(F32)) / span, -1.0, 1.0
        ).astype(BF16)

        @pl.when(sec < last)
        def _():
            y_forward(m).start()

        scaled[m] = ((xs[m] - mean) * inverse * gain_ref[...]).astype(BF16)

    def forward_tick(i, carry):
        @pl.when(i < MICRO)
        def _():
            forward_in(i)

        @pl.when(i == 1)
        def _():
            x_finish(0, UP)
            x_finish(1, UP)

        @pl.when(i >= 1)
        def _():
            forward_out(i - 1)

        return carry

    lax.fori_loop(0, MICRO + 1, forward_tick, 0)

    def b1(m):
        return move(u1s.at[m], u1r.at[m], b1send.at[m], b1recv.at[m], mate)

    def b2(m):
        return move(u2s.at[m], u2r.at[m], b2send.at[m], b2recv.at[m], far)

    def backward_in(m):
        @pl.when(sec == last)
        def _():
            gs[m] = exit_codes[m].astype(F32) * exit_scale[m]

        @pl.when(sec < last)
        def _():
            y_back(m).wait_recv()
            gs[m] = incb[m].astype(F32)

        rounded = gs[m].astype(BF16)
        gb[m] = rounded
        part = by_rows(rounded, weights(UP))
        u1s[m] = part
        b1(m).start()
        b1(m).wait_recv()
        u2s[m] = (part + u1r[m]).astype(BF16)
        b2(m).start()

    def backward_out(m):
        b2(m).wait_recv()
        grad_act = u2s[m].astype(F32) + u2r[m].astype(F32)
        pre = pres[m]
        bend = jnp.tanh(CURVE * (pre + 0.044715 * (pre * pre * pre)))
        slope = 0.5 * (1.0 + bend) + 0.5 * pre * (1.0 - bend * bend) * (
            CURVE * (1.0 + 3.0 * 0.044715 * pre * pre)
        )
        dpre = (grad_act * slope).astype(BF16)
        dpre_s[m] = dpre
        wide = dpre.astype(F32)
        mean_grad = jnp.sum(wide * gsum[...], 1, keepdims=True) / total
        mean_cross = jnp.sum(wide * pre, 1, keepdims=True) / total
        mean, inverse = norm_stat[m, 0], norm_stat[m, 1]
        normed = (xs[m] - mean) * inverse
        dn = times(dpre, weights(DOWN)) * gain_ref[...]
        dx = gs[m] + inverse * (dn - mean_grad - normed * mean_cross)
        gs[m] = dx
        dxb[m] = dx.astype(BF16)

        @pl.when(sec > 0)
        def _():
            y_back(m).start()

        return to_lanes(jnp.max(jnp.abs(dx), 1, keepdims=True), m * ROWS)

    peak_src[...] = jnp.zeros((8, 128), F32)

    def backward_tick(i, carry):
        backward_in(i)

        @pl.when(i >= 1)
        def _():
            peak_src[0:1] += backward_out(i - 1)

        return carry

    lax.fori_loop(0, MICRO, backward_tick, 0)

    def gradient(m, left, right):
        width = 256
        lhs = left[...].reshape(MICRO * ROWS, bot)

        def tile(i, carry):
            at = pl.ds(pl.multiple_of(i * width, width), width)
            rhs = right[:, :, at].reshape(MICRO * ROWS, width)
            gp[m, :, :, at] = by_cols(lhs, rhs).astype(BF16).reshape(NX, bot // NX, width)
            return carry

        lax.fori_loop(0, cols // width, tile, 0)

    low, high = slice(0, half), slice(half, cols)

    def gx_move(m, kind):
        src, dst, device = {
            0: (gp.at[m, xo, :, low], rx1.at[m, 0], to_right),
            1: (gp.at[m, xo, :, high], rx1.at[m, 1], to_left),
            2: (gp.at[m, xr, :, high], rx2.at[m, 0, :, high], to_right),
            3: (gp.at[m, xl, :, low], rx2.at[m, 1, :, low], to_left),
            4: (gp.at[m, xr, :, low], rx2.at[m, 0, :, low], to_right),
            5: (gp.at[m, xl, :, high], rx2.at[m, 1, :, high], to_left),
        }[kind]
        return move(src, dst, gxsend.at[m, kind], gxrecv.at[m, kind], device)

    def scatter_start(m):
        for kind in range(4):
            gx_move(m, kind).start()

    def scatter_forward(m):
        gx_move(m, 0).wait_recv()
        gp[m, xr, :, low] = (gp[m, xr, :, low].astype(F32) + rx1[m, 0].astype(F32)).astype(BF16)
        gx_move(m, 4).start()
        gx_move(m, 1).wait_recv()
        gp[m, xl, :, high] = (gp[m, xl, :, high].astype(F32) + rx1[m, 1].astype(F32)).astype(BF16)
        gx_move(m, 5).start()

    def scatter_sum(m):
        for kind in range(2, 6):
            gx_move(m, kind).wait_recv()
        own = gp[m, x].astype(F32) + rx2[m, 0].astype(F32) + rx2[m, 1].astype(F32)
        pick = spread_matrix(nz, unit).astype(BF16)
        zs[m] = by_cols(pick, own.astype(BF16)).astype(BF16).reshape(nz, PAD, cols)

    def gz_move(m, way, target):
        return move(
            zs.at[m, target], rz.at[m, way, target], gzsend.at[m, target],
            gzrecv.at[m, way, target], z_up if way == 0 else z_down,
        )

    def chain_step(k, carry):
        for m in (UP, DOWN):
            for way, target, wanted, fed in (
                (0, nz - 1 - k, nz - 1 - k > z, z > 0),
                (1, k, k < z, z < nz - 1),
            ):
                @pl.when(wanted)
                def _():
                    @pl.when(fed)
                    def _():
                        gz_move(m, way, target).wait_recv()
                        zs[m, target] = (
                            zs[m, target].astype(F32) + rz[m, way, target].astype(F32)
                        ).astype(BF16)

                    gz_move(m, way, target).start()

        return carry

    gradient(UP, hidden, gb)
    scatter_start(UP)
    peak_src[0:1] += backward_out(MICRO - 1)

    def peak_move(k):
        return move(peak_src, peak_in.at[k], peak_sem.at[0, k], peak_sem.at[1, k], others[k])

    for k in range(3):
        peak_move(k).start()
    gradient(DOWN, dpre_s, scaled)
    scatter_start(DOWN)
    scatter_forward(UP)
    scatter_forward(DOWN)
    scatter_sum(UP)
    scatter_sum(DOWN)
    lax.fori_loop(0, nz - 1, chain_step, 0)

    for k in range(3):
        peak_move(k).wait_recv()
    peak_row = jnp.maximum(
        jnp.maximum(peak_src[0:1], peak_in[0, 0:1]),
        jnp.maximum(peak_in[1, 0:1], peak_in[2, 0:1]),
    )
    peak_row = (peak_row + 1e-05).astype(BF16).astype(F32)

    def codes_back(m, carry):
        returned[m] = (gs[m] / to_column(peak_row, m * ROWS)).astype(BF16)
        return carry

    lax.fori_loop(0, MICRO, codes_back, 0)

    for m, out in ((UP, grad_up), (DOWN, grad_down)):
        out[...] = zs[m, z, 0:unit].astype(F32)
        for way, fed in ((0, z > 0), (1, z < nz - 1)):
            @pl.when(fed)
            def _():
                gz_move(m, way, z).wait_recv()
                out[...] += rz[m, way, z, 0:unit].astype(F32)

    for k in range(3):
        span_move(k).wait_send()
        peak_move(k).wait_send()

    def drain_micro(m, carry):
        for copy in l1(m) + l2(m) + (b1(m), b2(m)):
            copy.wait_send()

        @pl.when(sec < last)
        def _():
            y_forward(m).wait_send()

        @pl.when(sec > 0)
        def _():
            y_back(m).wait_send()

        return carry

    lax.fori_loop(0, MICRO, drain_micro, 0)

    for m in (DOWN, UP):
        for p in range(2):
            for kind in range(4):
                x_move(p, m, kind).wait_send()
        for kind in range(6):
            gx_move(m, kind).wait_send()

    def drain_z(slot, carry):
        for m in (DOWN, UP):
            @pl.when((z < nz - 1) & (slot <= z))
            def _():
                z_move(0, slot, m).wait_send()

            @pl.when((z > 0) & (slot >= z))
            def _():
                z_move(1, slot, m).wait_send()

            @pl.when(slot > z)
            def _():
                gz_move(m, 0, slot).wait_send()

            @pl.when(slot < z)
            def _():
                gz_move(m, 1, slot).wait_send()

        return carry

    lax.fori_loop(0, nz, drain_z, 0)


def solution(mesh):
    nz = mesh.shape["dp"] // NX

    def local(stored, entry, exit_codes, exit_scales, slot_ids, gain, down, up):
        unit, cols = down.shape[1], down.shape[2]
        bot = unit * mesh.shape["dp"]
        tokens = MICRO * ROWS
        pad = lambda w: jnp.pad(w, ((0, PAD - unit), (0, 0)))
        shard = jnp.stack([pad(down[0]), pad(up[0])])
        block = (MICRO, ROWS, cols)
        small = (MICRO, ROWS, bot)
        dma = pltpu.SemaphoreType.DMA
        vm = pltpu.VMEM
        xrows = bot // NX
        scratch = [
            vm((nz, 2, PAD, cols), BF16),
            vm((2, NX, 2, xrows // 2, cols), BF16),
            vm((8, 128), F32), vm((3, 8, 128), F32), vm((8, 128), F32),
            vm(block, BF16), vm(block, BF16),
            vm(block, F32),
            vm((MICRO, 2, ROWS, 1), F32),
            vm(block, BF16),
            vm(small, F32), vm(small, BF16),
            vm((1, bot), F32),
            vm(small, F32), vm(small, F32), vm((MICRO, 8, 128), F32), vm((MICRO, 8, 128), F32),
            vm(small, BF16), vm(small, BF16), vm((MICRO, 8, 128), F32), vm((MICRO, 8, 128), F32),
            vm(small, F32), vm(small, F32), vm(small, BF16), vm(small, BF16),
            vm(block, F32), vm(block, BF16), vm(small, BF16), vm(block, BF16),
            vm((8, 128), F32), vm((3, 8, 128), F32),
            vm((2, NX, xrows, cols), BF16),
            vm((2, 2, xrows, cols // 2), BF16),
            vm((2, 2, xrows, cols), BF16),
            vm((2, nz, PAD, cols), BF16),
            vm((2, 2, nz, PAD, cols), BF16),
            dma((2, 3)),
            dma((2, nz, 2)), dma((nz, 2)),
            dma((2, 2, 4)), dma((2, 2, 4)),
            dma((MICRO, 2)), dma((MICRO, 2)), dma((MICRO, 2)), dma((MICRO, 2)),
            dma((MICRO,)), dma((MICRO,)), dma((MICRO,)), dma((MICRO,)),
            dma((MICRO,)), dma((MICRO,)), dma((MICRO,)), dma((MICRO,)),
            dma((2, 3)),
            dma((2, 6)), dma((2, 6)),
            dma((2, nz)), dma((2, 2, nz)),
        ]
        in_vmem = pl.BlockSpec(memory_space=pltpu.VMEM)
        sent, returned, grad_down, grad_up = pl.pallas_call(
            lambda *refs: relay_kernel(nz, *refs),
            out_shape=(
                jax.ShapeDtypeStruct(block, BF16),
                jax.ShapeDtypeStruct(block, BF16),
                jax.ShapeDtypeStruct((unit, cols), F32),
                jax.ShapeDtypeStruct((unit, cols), F32),
            ),
            in_specs=[in_vmem] * 4 + [pl.BlockSpec(memory_space=pltpu.SMEM)] + [in_vmem] * 2,
            out_specs=(in_vmem,) * 4,
            scratch_shapes=scratch,
            compiler_params=pltpu.CompilerParams(
                collective_id=0, has_side_effects=True, vmem_limit_bytes=48 * 2**20
            ),
        )(
            stored[0].reshape(2, MICRO, ROWS, cols),
            entry.reshape(block),
            exit_codes.reshape(block),
            exit_scales.reshape(MICRO, ROWS, 1),
            slot_ids[0],
            gain,
            shard,
        )
        return (
            sent.reshape(1, tokens, cols),
            returned.reshape(1, tokens, cols),
            grad_down[None],
            grad_up[None],
        )

    in_specs = (
        P("section", None, "dp", "tensor"),
        P("dp", "tensor"),
        P("dp", "tensor"),
        P("dp"),
        P("dp", None),
        P("section", "tensor"),
        P("section", "dp", "tensor"),
        P("section", "dp", "tensor"),
    )
    out_specs = (P("section", "dp", "tensor"),) * 4
    return jax.shard_map(local, mesh=mesh, in_specs=in_specs, out_specs=out_specs, check_vma=False)
```

```python
import math

import jax
import jax.numpy as jnp
from jax import lax
from jax.experimental import pallas as pl
from jax.experimental.pallas import tpu as pltpu
from jax.sharding import PartitionSpec as P

MESH = pl.DeviceIdType.MESH
F32 = jnp.float32
BF16 = jnp.bfloat16
MICRO = 4
ROWS = 32
NX = 4
PAD = 16
DOWN, UP = 0, 1
CURVE = math.sqrt(2.0 / math.pi)


def by_rows(left, right):
    return lax.dot_general(left, right, (((1,), (1,)), ((), ())), preferred_element_type=F32)


def by_cols(left, right):
    return lax.dot_general(left, right, (((0,), (0,)), ((), ())), preferred_element_type=F32)


def times(left, right):
    return jnp.dot(left, right, preferred_element_type=F32)


def lane_mask(shift):
    row = lax.broadcasted_iota(jnp.int32, (ROWS, 128), 0)
    lane = lax.broadcasted_iota(jnp.int32, (ROWS, 128), 1)
    return lane == row + shift


def to_lanes(column, shift):
    return jnp.sum(jnp.where(lane_mask(shift), column, 0.0), 0, keepdims=True)


def to_column(lanes, shift):
    return jnp.sum(jnp.where(lane_mask(shift), lanes, 0.0), 1, keepdims=True)


def spread_matrix(shards, unit):
    shape = (shards * unit, shards * PAD)
    row = lax.broadcasted_iota(jnp.int32, shape, 0)
    col = lax.broadcasted_iota(jnp.int32, shape, 1)
    shard = jnp.zeros(shape, jnp.int32)
    for k in range(1, shards):
        shard += jnp.where(row >= k * unit, 1, 0)
    return jnp.where(col == shard * PAD + row - shard * unit, 1.0, 0.0)


def relay_kernel(
    nz, copies, entry, exit_codes, exit_scale, slots, gain_ref, shard,
    sent, returned, grad_down, grad_up,
    zbuf, wv, span_src, span_in, spans, incf, incb, xs, norm_stat, pres, gsum,
    p1s, p1r, t1s, t1r, p2s, p2r, t2s, t2r, u1s, u1r, u2s, u2r,
    gs, dxb, peak_src, peak_in, scaled, hidden, gb, dpre_s, pair_out, pair_in, own, zs, rz,
    span_sem, zsend, zrecv, xsend, xrecv, l1send, l1recv, l2send, l2recv,
    b1send, b1recv, b2send, b2recv, ysend, yrecv, wsend, wrecv, peak_sem,
    fsend, frecv, psend, precv, gzsend, gzrecv,
):
    sec = lax.axis_index("section")
    last = lax.axis_size("section") - 1
    dp = lax.axis_index("dp")
    ten = lax.axis_index("tensor")
    x = dp // nz
    z = dp % nz
    half_z = nz // 2
    unit = grad_down.shape[0]
    cols = gain_ref.shape[1]
    half = cols // 2
    bot = pres.shape[2]
    total = cols * 4
    xr, xl, xo = (x + 1) % NX, (x + NX - 1) % NX, (x + 2) % NX
    to_right = {"dp": xr * nz + z}
    to_left = {"dp": xl * nz + z}
    mate = {"tensor": ten + 1 - 2 * (ten % 2)}
    far = {"tensor": (ten + 2) % 4}
    others = [{"tensor": (ten + k) % 4} for k in (1, 2, 3)]
    next_sec = {"section": (sec + 1) % (last + 1)}
    prev_sec = {"section": (sec + last) % (last + 1)}
    z_up = {"dp": x * nz + (z + 1) % nz}
    z_down = {"dp": x * nz + (z + nz - 1) % nz}

    barrier = pltpu.get_barrier_semaphore()
    x_peers = [{"dp": (x + k) % NX * nz + z} for k in (1, 2, 3)]
    z_peers = [{"dp": x * nz + (z + 2 * k) % nz} for k in (1, 2, 3)]
    z_mate = {"dp": dp + 1 - 2 * (z % 2)}
    friends = others + [next_sec, prev_sec, z_up, z_down] + x_peers + z_peers
    for friend in friends:
        pl.semaphore_signal(barrier, inc=1, device_id=friend, device_id_type=MESH)
    pl.semaphore_wait(barrier, len(friends))

    def move(src, dst, send, recv, device):
        return pltpu.make_async_remote_copy(
            src_ref=src, dst_ref=dst, send_sem=send, recv_sem=recv,
            device_id=device, device_id_type=MESH,
        )

    def z_move(way, slot, m):
        return move(
            zbuf.at[slot, m], zbuf.at[slot, m], zsend.at[way, slot, m], zrecv.at[slot, m],
            z_up if way == 0 else z_down,
        )

    def z_step(k):
        for m in (DOWN, UP):
            @pl.when(z - k >= 0)
            def _():
                z_move(0, z - k, m).wait_recv()

                @pl.when(z < nz - 1)
                def _():
                    z_move(0, z - k, m).start()

            @pl.when(z + k < nz)
            def _():
                z_move(1, z + k, m).wait_recv()

                @pl.when(z > 0)
                def _():
                    z_move(1, z + k, m).start()

    def z_steps(first, end):
        def step(k, carry):
            z_step(k)
            return carry

        lax.fori_loop(first, end, step, 0)

    group = [z // half_z, 1 - z // half_z]

    def x_move(p, m, kind):
        g = group[p]
        block, device, part = {
            0: (x, to_right, slice(None)),
            1: (x, to_left, slice(None)),
            2: (xl, to_right, slice(0, half)),
            3: (xr, to_left, slice(half, cols)),
        }[kind]
        ref = wv.at[m, block, g] if kind < 2 else wv.at[m, block, g, :, part]
        return move(ref, ref, xsend.at[p, m, kind], xrecv.at[p, m, kind], device)

    def x_arrival(p, m, kind):
        g = group[p]
        ref = {
            0: lambda: wv.at[m, xl, g],
            1: lambda: wv.at[m, xr, g],
            2: lambda: wv.at[m, xo, g, :, slice(0, half)],
            3: lambda: wv.at[m, xo, g, :, slice(half, cols)],
        }[kind]()
        move(ref, ref, xsend.at[p, m, kind], xrecv.at[p, m, kind], to_right).wait_recv()

    def x_own(p, m):
        block = zbuf[pl.ds(group[p] * half_z, half_z), m].reshape(half_z * PAD, cols)
        pick = spread_matrix(half_z, unit).astype(BF16)
        wv[m, x, group[p]] = times(pick, block).astype(BF16)
        x_move(p, m, 0).start()
        x_move(p, m, 1).start()

    def x_forward(p, m):
        x_arrival(p, m, 0)
        x_move(p, m, 2).start()
        x_arrival(p, m, 1)
        x_move(p, m, 3).start()

    def x_finish(p, m):
        x_arrival(p, m, 2)
        x_arrival(p, m, 3)

    zbuf[z] = shard[...]

    for m in (DOWN, UP):
        @pl.when(z < nz - 1)
        def _():
            z_move(0, z, m).start()

        @pl.when(z > 0)
        def _():
            z_move(1, z, m).start()

    @pl.when(sec == 0)
    def _():
        incf[...] = entry[...]

    def squares(m, carry):
        sums = []
        for k in range(2):
            rows = copies[k, slots[m]].astype(F32)
            sums.append(to_lanes(jnp.sum(rows * rows, 1, keepdims=True), m * ROWS))
        return carry[0] + sums[0], carry[1] + sums[1]

    nothing = jnp.zeros((1, 128), F32)
    square_in, square_out = lax.fori_loop(0, MICRO, squares, (nothing, nothing))
    span_src[...] = jnp.zeros((8, 128), F32)
    span_src[0:1] = square_in
    span_src[1:2] = square_out

    def span_move(k):
        return move(span_src, span_in.at[k], span_sem.at[0, k], span_sem.at[1, k], others[k])

    for k in range(3):
        span_move(k).start()

    z_steps(1, half_z)
    for m in (DOWN, UP):
        x_own(0, m)
    z_steps(half_z, half_z + 2)
    x_forward(0, DOWN)
    z_steps(half_z + 2, half_z + 3)
    x_forward(0, UP)
    z_steps(half_z + 3, nz)
    for m in (DOWN, UP):
        x_own(1, m)
    for k in range(3):
        span_move(k).wait_recv()
    spans[...] = 2.0 * jnp.sqrt(
        (span_src[...] + span_in[0] + span_in[1] + span_in[2]) / total + 1e-05
    )
    for m in (DOWN, UP):
        x_forward(1, m)
    x_finish(0, DOWN)
    x_finish(1, DOWN)

    def weights(m):
        return wv[m].reshape(bot, cols)

    gain = gain_ref[...]
    first = gain.astype(BF16).astype(F32)
    second = (gain - first).astype(BF16).astype(F32)
    third = gain - first - second
    row = lax.broadcasted_iota(jnp.int32, (PAD, cols), 0)
    terms = jnp.where(
        row == 0, first, jnp.where(row == 1, second, jnp.where(row == 2, third, 0.0))
    ).astype(BF16)
    gain_down = jnp.sum(by_rows(terms, weights(DOWN)), 0, keepdims=True)
    pieces = bot // 128

    def put_stat(ref, m, mean, spread, gd):
        ref[m] = jnp.zeros((8, 128), F32)
        ref[m, 0:1] = to_lanes(mean, 0)
        ref[m, 1:2] = to_lanes(spread, 0)
        for i in range(pieces):
            ref[m, 2 + i : 3 + i] = gd[:, i * 128 : (i + 1) * 128]

    def get_stat(ref, m):
        gd = jnp.concatenate([ref[m, 2 + i : 3 + i] for i in range(pieces)], axis=1)
        return to_column(ref[m, 0:1], 0), to_column(ref[m, 1:2], 0), gd

    def join(count, p, mean, spread, gd, p_other, mean_other, spread_other, gd_other):
        both = 0.5 * (mean + mean_other)
        mine, theirs = mean - both, mean_other - both
        spread_both = spread + spread_other + count * (mine * mine + theirs * theirs)
        p_both = (p + p_other) + (mine * gd + theirs * gd_other)
        return p_both, both, spread_both, gd + gd_other

    def l1(m):
        return (
            move(p1s.at[m], p1r.at[m], l1send.at[m, 0], l1recv.at[m, 0], mate),
            move(t1s.at[m], t1r.at[m], l1send.at[m, 1], l1recv.at[m, 1], mate),
        )

    def l2(m):
        return (
            move(p2s.at[m], p2r.at[m], l2send.at[m, 0], l2recv.at[m, 0], far),
            move(t2s.at[m], t2r.at[m], l2send.at[m, 1], l2recv.at[m, 1], far),
        )

    def y_forward(m):
        return move(sent.at[m], incf.at[m], ysend.at[m], yrecv.at[m], next_sec)

    def y_back(m):
        return move(dxb.at[m], incb.at[m], wsend.at[m], wrecv.at[m], prev_sec)

    def each(step):
        def tick(m, carry):
            step(m)
            return carry

        lax.fori_loop(0, MICRO, tick, 0)

    factors = (scaled, hidden, gb, dpre_s)

    def factor_move(which, m, k):
        ref = factors[which].at[x, m]
        return move(ref, ref, fsend.at[which, m, k], frecv.at[which, m, k], x_peers[k])

    def factor_send(which, m):
        for k in range(3):
            factor_move(which, m, k).start()

    def factor_wait(which):
        def wait(m):
            for k in range(3):
                ref = factors[which].at[(x + NX - 1 - k) % NX, m]
                move(ref, ref, fsend.at[which, m, k], frecv.at[which, m, k], x_peers[k]).wait_recv()

        each(wait)

    def forward_in(m):
        @pl.when(sec > 0)
        def _():
            y_forward(m).wait_recv()

        span = to_column(spans[0:1], m * ROWS)
        rows = copies[0, slots[m]].astype(F32) + span * incf[m].astype(F32)
        xs[m] = rows
        mean = jnp.sum(rows, 1, keepdims=True) / cols
        centred = rows - mean
        spread = jnp.sum(centred * centred, 1, keepdims=True)
        part = by_rows((centred * gain_ref[...]).astype(BF16), weights(DOWN))
        p1s[m] = part
        put_stat(t1s, m, mean, spread, gain_down)
        for copy in l1(m):
            copy.start()
        for copy in l1(m):
            copy.wait_recv()
        part, mean, spread, gd = join(
            float(cols), part, mean, spread, gain_down, p1r[m], *get_stat(t1r, m)
        )
        p2s[m] = part.astype(BF16)
        put_stat(t2s, m, mean, spread, gd)
        for copy in l2(m):
            copy.start()

    def forward_out(m):
        for copy in l2(m):
            copy.wait_recv()
        raw, mean, spread, gd = join(
            float(2 * cols), p2s[m].astype(F32), *get_stat(t2s, m),
            p2r[m].astype(F32), *get_stat(t2r, m)
        )
        inverse = lax.rsqrt(spread / total + 1e-05)
        pre = raw * inverse
        gsum[...] = gd
        pres[m] = pre
        norm_stat[m, 0] = mean
        norm_stat[m, 1] = inverse
        act = (0.5 * pre * (1.0 + jnp.tanh(CURVE * (pre + 0.044715 * (pre * pre * pre))))).astype(BF16)
        hidden[x, m] = act
        result = xs[m] + times(act, weights(UP))
        span = to_column(spans[1:2], m * ROWS)
        sent[m] = jnp.clip(
            (result - copies[1, slots[m]].astype(F32)) / span, -1.0, 1.0
        ).astype(BF16)

        @pl.when(sec < last)
        def _():
            y_forward(m).start()

        scaled[x, m] = ((xs[m] - mean) * inverse * gain_ref[...]).astype(BF16)
        factor_send(0, m)
        factor_send(1, m)

    def b1(m):
        return move(u1s.at[m], u1r.at[m], b1send.at[m], b1recv.at[m], mate)

    def b2(m):
        return move(u2s.at[m], u2r.at[m], b2send.at[m], b2recv.at[m], far)

    def backward_in(m):
        @pl.when(sec == last)
        def _():
            gs[m] = exit_codes[m].astype(F32) * exit_scale[m]

        @pl.when(sec < last)
        def _():
            y_back(m).wait_recv()
            gs[m] = incb[m].astype(F32)

        rounded = gs[m].astype(BF16)
        gb[x, m] = rounded
        part = by_rows(rounded, weights(UP))
        u1s[m] = part
        b1(m).start()
        b1(m).wait_recv()
        u2s[m] = (part + u1r[m]).astype(BF16)
        b2(m).start()
        factor_send(2, m)

    def backward_out(m):
        b2(m).wait_recv()
        grad_act = u2s[m].astype(F32) + u2r[m].astype(F32)
        pre = pres[m]
        bend = jnp.tanh(CURVE * (pre + 0.044715 * (pre * pre * pre)))
        slope = 0.5 * (1.0 + bend) + 0.5 * pre * (1.0 - bend * bend) * (
            CURVE * (1.0 + 3.0 * 0.044715 * pre * pre)
        )
        dpre = (grad_act * slope).astype(BF16)
        dpre_s[x, m] = dpre
        factor_send(3, m)
        wide = dpre.astype(F32)
        mean_grad = jnp.sum(wide * gsum[...], 1, keepdims=True) / total
        mean_cross = jnp.sum(wide * pre, 1, keepdims=True) / total
        mean, inverse = norm_stat[m, 0], norm_stat[m, 1]
        normed = (xs[m] - mean) * inverse
        dn = times(dpre, weights(DOWN)) * gain_ref[...]
        dx = gs[m] + inverse * (dn - mean_grad - normed * mean_cross)
        gs[m] = dx
        dxb[m] = dx.astype(BF16)

        @pl.when(sec > 0)
        def _():
            y_back(m).start()

        peak_src[0:1] += to_lanes(jnp.max(jnp.abs(dx), 1, keepdims=True), m * ROWS)

    peak_src[...] = jnp.zeros((8, 128), F32)

    @pl.when(sec == last)
    def _():
        x_finish(0, UP)
        x_finish(1, UP)
        each(backward_in)

    each(forward_in)

    @pl.when(sec < last)
    def _():
        x_finish(0, UP)
        x_finish(1, UP)

    def forward_end(m):
        forward_out(m)

        @pl.when(sec == last)
        def _():
            backward_out(m)

    each(forward_end)

    @pl.when(sec < last)
    def _():
        each(backward_in)

        def tick(m, carry):
            backward_out(m)
            return carry

        lax.fori_loop(0, MICRO - 1, tick, 0)

    quarter = nz // 2
    parity = z % 2

    def unit_pick(side):
        shape = (bot, quarter * unit)
        row = lax.broadcasted_iota(jnp.int32, shape, 0)
        col = lax.broadcasted_iota(jnp.int32, shape, 1)
        source = col + (x * nz + side) * unit
        for k in range(1, quarter):
            source += jnp.where(col >= k * unit, unit, 0)
        return jnp.where(row == source, 1.0, 0.0).astype(BF16)

    def gradient(p, side):
        left, right = (hidden, gb) if p < 2 else (dpre_s, scaled)
        tokens = NX * MICRO * ROWS
        at = slice(p % 2 * half, (p % 2 + 1) * half)
        lhs = times(left[...].reshape(tokens, bot), unit_pick(side)).astype(BF16)
        return by_cols(lhs, right[:, :, :, at].reshape(tokens, half))

    def pair_move(p):
        return move(pair_out.at[p], pair_in.at[p], psend.at[p], precv.at[p], z_mate)

    def gz_move(p, k):
        slot = (z + 2 * (k + 1)) % nz // 2
        return move(zs.at[p, slot], rz.at[p, k], gzsend.at[p, k], gzrecv.at[p, k], z_peers[k])

    def gradient_first(pieces):
        for p in pieces:
            pair_out[p] = gradient(p, 1 - parity).astype(BF16)
            pair_move(p).start()
        for p in pieces:
            own[p] = gradient(p, parity)

    def gradient_second(p):
        pair_move(p).wait_recv()
        both = (own[p] + pair_in[p].astype(F32)).astype(BF16)
        pad = spread_matrix(quarter, unit).astype(BF16)
        zs[p] = by_cols(pad, both).astype(BF16).reshape(quarter, PAD, half)
        for k in range(3):
            gz_move(p, k).start()

    @pl.when(sec < last)
    def _():
        backward_out(MICRO - 1)

    def peak_move(k):
        return move(peak_src, peak_in.at[k], peak_sem.at[0, k], peak_sem.at[1, k], others[k])

    for k in range(3):
        peak_move(k).start()
    factor_wait(1)
    factor_wait(2)
    gradient_first((0, 1))
    factor_wait(0)
    factor_wait(3)
    gradient_first((2, 3))
    for p in range(4):
        gradient_second(p)

    for k in range(3):
        peak_move(k).wait_recv()
    peak_row = jnp.maximum(
        jnp.maximum(peak_src[0:1], peak_in[0, 0:1]),
        jnp.maximum(peak_in[1, 0:1], peak_in[2, 0:1]),
    )
    peak_row = (peak_row + 1e-05).astype(BF16).astype(F32)

    def codes_back(m):
        returned[m] = (gs[m] / to_column(peak_row, m * ROWS)).astype(BF16)

    each(codes_back)

    for p in range(4):
        out = grad_up if p < 2 else grad_down
        at = slice(p % 2 * half, (p % 2 + 1) * half)
        result = zs[p, z // 2].astype(F32)
        for k in range(3):
            gz_move(p, k).wait_recv()
            result += rz[p, k].astype(F32)
        out[:, at] = result[0:unit]

    for k in range(3):
        span_move(k).wait_send()
        peak_move(k).wait_send()

    def drain_micro(m, carry):
        for copy in l1(m) + l2(m) + (b1(m), b2(m)):
            copy.wait_send()

        @pl.when(sec < last)
        def _():
            y_forward(m).wait_send()

        @pl.when(sec > 0)
        def _():
            y_back(m).wait_send()

        return carry

    lax.fori_loop(0, MICRO, drain_micro, 0)

    for m in (DOWN, UP):
        for p in range(2):
            for kind in range(4):
                x_move(p, m, kind).wait_send()

    for p in range(4):
        pair_move(p).wait_send()
        for k in range(3):
            gz_move(p, k).wait_send()

    def drain_factors(m):
        for which in range(4):
            for k in range(3):
                factor_move(which, m, k).wait_send()

    each(drain_factors)

    def drain_z(slot, carry):
        for m in (DOWN, UP):
            @pl.when((z < nz - 1) & (slot <= z))
            def _():
                z_move(0, slot, m).wait_send()

            @pl.when((z > 0) & (slot >= z))
            def _():
                z_move(1, slot, m).wait_send()

        return carry

    lax.fori_loop(0, nz, drain_z, 0)


def solution(mesh):
    nz = mesh.shape["dp"] // NX

    def local(stored, entry, exit_codes, exit_scales, slot_ids, gain, down, up):
        unit, cols = down.shape[1], down.shape[2]
        bot = unit * mesh.shape["dp"]
        tokens = MICRO * ROWS
        pad = lambda w: jnp.pad(w, ((0, PAD - unit), (0, 0)))
        shard = jnp.stack([pad(down[0]), pad(up[0])])
        block = (MICRO, ROWS, cols)
        small = (MICRO, ROWS, bot)
        dma = pltpu.SemaphoreType.DMA
        vm = pltpu.VMEM
        xrows = bot // NX
        scratch = [
            vm((nz, 2, PAD, cols), BF16),
            vm((2, NX, 2, xrows // 2, cols), BF16),
            vm((8, 128), F32), vm((3, 8, 128), F32), vm((8, 128), F32),
            vm(block, BF16), vm(block, BF16),
            vm(block, F32),
            vm((MICRO, 2, ROWS, 1), F32),
            vm(small, F32),
            vm((1, bot), F32),
            vm(small, F32), vm(small, F32), vm((MICRO, 8, 128), F32), vm((MICRO, 8, 128), F32),
            vm(small, BF16), vm(small, BF16), vm((MICRO, 8, 128), F32), vm((MICRO, 8, 128), F32),
            vm(small, F32), vm(small, F32), vm(small, BF16), vm(small, BF16),
            vm(block, F32), vm(block, BF16),
            vm((8, 128), F32), vm((3, 8, 128), F32),
            vm((NX, *block), BF16), vm((NX, *small), BF16),
            vm((NX, *block), BF16), vm((NX, *small), BF16),
            vm((4, xrows // 2, cols // 2), BF16), vm((4, xrows // 2, cols // 2), BF16),
            vm((4, xrows // 2, cols // 2), F32),
            vm((4, nz // 2, PAD, cols // 2), BF16),
            vm((4, 3, PAD, cols // 2), BF16),
            dma((2, 3)),
            dma((2, nz, 2)), dma((nz, 2)),
            dma((2, 2, 4)), dma((2, 2, 4)),
            dma((MICRO, 2)), dma((MICRO, 2)), dma((MICRO, 2)), dma((MICRO, 2)),
            dma((MICRO,)), dma((MICRO,)), dma((MICRO,)), dma((MICRO,)),
            dma((MICRO,)), dma((MICRO,)), dma((MICRO,)), dma((MICRO,)),
            dma((2, 3)),
            dma((4, MICRO, 3)), dma((4, MICRO, 3)),
            dma((4,)), dma((4,)),
            dma((4, 3)), dma((4, 3)),
        ]
        in_vmem = pl.BlockSpec(memory_space=pltpu.VMEM)
        sent, returned, grad_down, grad_up = pl.pallas_call(
            lambda *refs: relay_kernel(nz, *refs),
            out_shape=(
                jax.ShapeDtypeStruct(block, BF16),
                jax.ShapeDtypeStruct(block, BF16),
                jax.ShapeDtypeStruct((unit, cols), F32),
                jax.ShapeDtypeStruct((unit, cols), F32),
            ),
            in_specs=[in_vmem] * 4 + [pl.BlockSpec(memory_space=pltpu.SMEM)] + [in_vmem] * 2,
            out_specs=(in_vmem,) * 4,
            scratch_shapes=scratch,
            compiler_params=pltpu.CompilerParams(
                collective_id=0, has_side_effects=True, vmem_limit_bytes=48 * 2**20
            ),
        )(
            stored[0].reshape(2, MICRO, ROWS, cols),
            entry.reshape(block),
            exit_codes.reshape(block),
            exit_scales.reshape(MICRO, ROWS, 1),
            slot_ids[0],
            gain,
            shard,
        )
        return (
            sent.reshape(1, tokens, cols),
            returned.reshape(1, tokens, cols),
            grad_down[None],
            grad_up[None],
        )

    in_specs = (
        P("section", None, "dp", "tensor"),
        P("dp", "tensor"),
        P("dp", "tensor"),
        P("dp"),
        P("dp", None),
        P("section", "tensor"),
        P("section", "dp", "tensor"),
        P("section", "dp", "tensor"),
    )
    out_specs = (P("section", "dp", "tensor"),) * 4
    return jax.shard_map(local, mesh=mesh, in_specs=in_specs, out_specs=out_specs, check_vma=False)
```

```python
import math

import jax
import jax.numpy as jnp
from jax import lax
from jax.experimental import pallas as pl
from jax.experimental.pallas import tpu as pltpu
from jax.sharding import PartitionSpec as P

MESH = pl.DeviceIdType.MESH
F32 = jnp.float32
BF16 = jnp.bfloat16
MICRO = 4
ROWS = 32
NX = 4
PAD = 16
DOWN, UP, NEXT_DOWN, PREV_UP = ALL = (0, 1, 2, 3)
OWN, HOP = 0, 1
CURVE = math.sqrt(2.0 / math.pi)


def by_rows(left, right):
    return lax.dot_general(left, right, (((1,), (1,)), ((), ())), preferred_element_type=F32)


def by_cols(left, right):
    return lax.dot_general(left, right, (((0,), (0,)), ((), ())), preferred_element_type=F32)


def times(left, right):
    return jnp.dot(left, right, preferred_element_type=F32)


def lane_mask(shift):
    row = lax.broadcasted_iota(jnp.int32, (ROWS, 128), 0)
    lane = lax.broadcasted_iota(jnp.int32, (ROWS, 128), 1)
    return lane == row + shift


def to_lanes(column, shift):
    return jnp.sum(jnp.where(lane_mask(shift), column, 0.0), 0, keepdims=True)


def to_column(lanes, shift):
    return jnp.sum(jnp.where(lane_mask(shift), lanes, 0.0), 1, keepdims=True)


def spread_matrix(shards, unit):
    shape = (shards * unit, shards * PAD)
    row = lax.broadcasted_iota(jnp.int32, shape, 0)
    col = lax.broadcasted_iota(jnp.int32, shape, 1)
    shard = jnp.zeros(shape, jnp.int32)
    for k in range(1, shards):
        shard += jnp.where(row >= k * unit, 1, 0)
    return jnp.where(col == shard * PAD + row - shard * unit, 1.0, 0.0)


def relay_kernel(
    nz, copies, entry, exit_codes, exit_scale, slots, gain_ref, shard,
    sent, returned, grad_down, grad_up,
    zbuf, wv, span_src, span_in, spans, incf, incb, xs, norm_stat, pres, gsum,
    own_gain_down, next_gain_down, next_gain,
    p1s, p1r, t1s, t1r, p2s, p2r, t2s, t2r, u1s, u1r, u2s, u2r,
    gs, dxb, peak_src, peak_in, scaled, hidden, gb, dpre_s, pair_out, pair_in, own, zs, rz,
    span_sem, ssend, srecv, zsend, zrecv, xsend, xrecv, l1send, l1recv, l2send, l2recv,
    b1send, b1recv, b2send, b2recv, ysend, yrecv, wsend, wrecv, peak_sem,
    fsend, frecv, psend, precv, gzsend, gzrecv,
):
    sec = lax.axis_index("section")
    last = lax.axis_size("section") - 1
    dp = lax.axis_index("dp")
    ten = lax.axis_index("tensor")
    x = dp // nz
    z = dp % nz
    half_z = nz // 2
    unit = grad_down.shape[0]
    cols = gain_ref.shape[1]
    half = cols // 2
    bot = pres.shape[2]
    total = cols * 4
    xr, xl, xo = (x + 1) % NX, (x + NX - 1) % NX, (x + 2) % NX
    to_right = {"dp": xr * nz + z}
    to_left = {"dp": xl * nz + z}
    mate = {"tensor": ten + 1 - 2 * (ten % 2)}
    far = {"tensor": (ten + 2) % 4}
    others = [{"tensor": (ten + k) % 4} for k in (1, 2, 3)]
    next_sec = {"section": (sec + 1) % (last + 1)}
    prev_sec = {"section": (sec + last) % (last + 1)}
    z_up = {"dp": x * nz + (z + 1) % nz}
    z_down = {"dp": x * nz + (z + nz - 1) % nz}

    barrier = pltpu.get_barrier_semaphore()
    x_peers = [{"dp": (x + k) % NX * nz + z} for k in (1, 2, 3)]
    z_peers = [{"dp": x * nz + (z + 2 * k) % nz} for k in (1, 2, 3)]
    z_mate = {"dp": dp + 1 - 2 * (z % 2)}
    diagonal = [{"section": to["section"], "tensor": far["tensor"]} for to in (next_sec, prev_sec)]
    friends = others + [next_sec, prev_sec, z_up, z_down] + x_peers + z_peers + diagonal
    for friend in friends:
        pl.semaphore_signal(barrier, inc=1, device_id=friend, device_id_type=MESH)
    pl.semaphore_wait(barrier, len(friends))

    def move(src, dst, send, recv, device):
        return pltpu.make_async_remote_copy(
            src_ref=src, dst_ref=dst, send_sem=send, recv_sem=recv,
            device_id=device, device_id_type=MESH,
        )

    def each(step):
        def tick(m, carry):
            step(m)
            return carry

        lax.fori_loop(0, MICRO, tick, 0)

    has = {DOWN: None, UP: None, NEXT_DOWN: sec < last, PREV_UP: sec > 0}

    def if_has(m, step):
        if has[m] is None:
            step()
        else:
            pl.when(has[m])(step)

    def shard_move(m):
        if m == NEXT_DOWN:
            return move(shard.at[DOWN], zbuf.at[z, m], ssend.at[0], srecv.at[0], prev_sec)
        if m == PREV_UP:
            return move(shard.at[UP], zbuf.at[z, m], ssend.at[1], srecv.at[1], next_sec)
        return move(gain_ref, next_gain, ssend.at[2], srecv.at[2], prev_sec)

    def z_move(way, slot, m):
        return move(
            zbuf.at[slot, m], zbuf.at[slot, m], zsend.at[way, slot, m], zrecv.at[slot, m],
            z_up if way == 0 else z_down,
        )

    def z_begin(m):
        @pl.when(z < nz - 1)
        def _():
            z_move(0, z, m).start()

        @pl.when(z > 0)
        def _():
            z_move(1, z, m).start()

    def z_step(k):
        for m in ALL:
            def pass_on():
                @pl.when(z - k >= 0)
                def _():
                    z_move(0, z - k, m).wait_recv()

                    @pl.when(z < nz - 1)
                    def _():
                        z_move(0, z - k, m).start()

                @pl.when(z + k < nz)
                def _():
                    z_move(1, z + k, m).wait_recv()

                    @pl.when(z > 0)
                    def _():
                        z_move(1, z + k, m).start()

            if_has(m, pass_on)

    def z_steps(first, end):
        def step(k, carry):
            z_step(k)
            return carry

        lax.fori_loop(first, end, step, 0)

    group = [z // half_z, 1 - z // half_z]

    def x_move(p, m, kind):
        g = group[p]
        block, device, part = {
            0: (x, to_right, slice(None)),
            1: (x, to_left, slice(None)),
            2: (xl, to_right, slice(0, half)),
            3: (xr, to_left, slice(half, cols)),
        }[kind]
        ref = wv.at[m, block, g] if kind < 2 else wv.at[m, block, g, :, part]
        return move(ref, ref, xsend.at[p, m, kind], xrecv.at[p, m, kind], device)

    def x_arrival(p, m, kind):
        g = group[p]
        ref = {
            0: lambda: wv.at[m, xl, g],
            1: lambda: wv.at[m, xr, g],
            2: lambda: wv.at[m, xo, g, :, slice(0, half)],
            3: lambda: wv.at[m, xo, g, :, slice(half, cols)],
        }[kind]()
        move(ref, ref, xsend.at[p, m, kind], xrecv.at[p, m, kind], to_right).wait_recv()

    def x_own(p, m):
        block = zbuf[pl.ds(group[p] * half_z, half_z), m].reshape(half_z * PAD, cols)
        pick = spread_matrix(half_z, unit).astype(BF16)
        wv[m, x, group[p]] = times(pick, block).astype(BF16)
        x_move(p, m, 0).start()
        x_move(p, m, 1).start()

    def x_forward(p, m):
        x_arrival(p, m, 0)
        x_move(p, m, 2).start()
        x_arrival(p, m, 1)
        x_move(p, m, 3).start()

    def x_finish(m):
        for p in range(2):
            x_arrival(p, m, 2)
            x_arrival(p, m, 3)

    @pl.when(sec > 0)
    def _():
        shard_move(NEXT_DOWN).start()
        shard_move(None).start()

    @pl.when(sec < last)
    def _():
        shard_move(PREV_UP).start()

    for m in (DOWN, UP):
        zbuf[z, m] = shard[m]
        z_begin(m)

    def squares(m, carry):
        sums = []
        for k in range(2):
            rows = copies[k, slots[m]].astype(F32)
            sums.append(to_lanes(jnp.sum(rows * rows, 1, keepdims=True), m * ROWS))
        return carry[0] + sums[0], carry[1] + sums[1]

    nothing = jnp.zeros((1, 128), F32)
    square_in, square_out = lax.fori_loop(0, MICRO, squares, (nothing, nothing))
    span_src[...] = jnp.zeros((8, 128), F32)
    span_src[0:1] = square_in
    span_src[1:2] = square_out

    def span_move(k):
        return move(span_src, span_in.at[k], span_sem.at[0, k], span_sem.at[1, k], others[k])

    for k in range(3):
        span_move(k).start()

    @pl.when(sec < last)
    def _():
        shard_move(NEXT_DOWN).wait_recv()
        z_begin(NEXT_DOWN)

    @pl.when(sec > 0)
    def _():
        shard_move(PREV_UP).wait_recv()
        z_begin(PREV_UP)

    z_steps(1, half_z)
    for m in (DOWN, UP, NEXT_DOWN):
        if_has(m, lambda: x_own(0, m))
    z_steps(half_z, half_z + 2)
    x_forward(0, DOWN)
    z_steps(half_z + 2, half_z + 3)
    x_forward(0, UP)
    z_steps(half_z + 3, nz)
    for m in (DOWN, UP, NEXT_DOWN):
        if_has(m, lambda: x_own(1, m))
    if_has(NEXT_DOWN, lambda: x_forward(0, NEXT_DOWN))
    for p in range(2):
        if_has(PREV_UP, lambda: x_own(p, PREV_UP))
    for k in range(3):
        span_move(k).wait_recv()
    spans[...] = 2.0 * jnp.sqrt(
        (span_src[...] + span_in[0] + span_in[1] + span_in[2]) / total + 1e-05
    )
    x_forward(1, DOWN)
    x_forward(1, UP)
    x_finish(DOWN)

    def weights(m):
        return wv[m].reshape(bot, cols)

    def gain_times(gain, m):
        first = gain.astype(BF16).astype(F32)
        second = (gain - first).astype(BF16).astype(F32)
        third = gain - first - second
        row = lax.broadcasted_iota(jnp.int32, (PAD, cols), 0)
        terms = jnp.where(
            row == 0, first, jnp.where(row == 1, second, jnp.where(row == 2, third, 0.0))
        ).astype(BF16)
        return jnp.sum(by_rows(terms, weights(m)), 0, keepdims=True)

    pieces = bot // 128

    def put_stat(ref, mean, spread, gd):
        ref[...] = jnp.zeros((8, 128), F32)
        ref[0:1] = to_lanes(mean, 0)
        ref[1:2] = to_lanes(spread, 0)
        for i in range(pieces):
            ref[2 + i : 3 + i] = gd[:, i * 128 : (i + 1) * 128]

    def get_stat(ref):
        gd = jnp.concatenate([ref[2 + i : 3 + i] for i in range(pieces)], axis=1)
        return to_column(ref[0:1], 0), to_column(ref[1:2], 0), gd

    def join(count, p, mean, spread, gd, p_other, mean_other, spread_other, gd_other):
        both = 0.5 * (mean + mean_other)
        mine, theirs = mean - both, mean_other - both
        spread_both = spread + spread_other + count * (mine * mine + theirs * theirs)
        p_both = (p + p_other) + (mine * gd + theirs * gd_other)
        return p_both, both, spread_both, gd + gd_other

    far_of, far_before = diagonal

    def l1(step, m):
        return [
            move(src.at[step, m], dst.at[step, m], l1send.at[step, m, i], l1recv.at[step, m, i], mate)
            for i, (src, dst) in enumerate(((p1s, p1r), (t1s, t1r)))
        ]

    def l2(step, m):
        places = [(1, far)] if step == OWN else [(0, next_sec), (1, far_of)]
        return [
            move(
                src.at[step, m], dst.at[place, m], l2send.at[step, m, i, place],
                l2recv.at[m, i, place], device,
            )
            for i, (src, dst) in enumerate(((p2s, p2r), (t2s, t2r)))
            for place, device in places
        ]

    def y_forward(m):
        return move(sent.at[m], incf.at[m], ysend.at[m], yrecv.at[m], next_sec)

    def y_back(m):
        return move(dxb.at[m], incb.at[m], wsend.at[m], wrecv.at[m], prev_sec)

    factors = (scaled, hidden, gb, dpre_s)

    def factor_move(which, m, k):
        ref = factors[which].at[x, m]
        return move(ref, ref, fsend.at[which, m, k], frecv.at[which, m, k], x_peers[k])

    def factor_send(which, m):
        for k in range(3):
            factor_move(which, m, k).start()

    def factor_wait(which):
        def wait(m):
            for k in range(3):
                ref = factors[which].at[(x + NX - 1 - k) % NX, m]
                move(ref, ref, fsend.at[which, m, k], frecv.at[which, m, k], x_peers[k]).wait_recv()

        each(wait)

    def enter_begin(step, m, rows, gain, gd, w):
        mean = jnp.sum(rows, 1, keepdims=True) / cols
        centred = rows - mean
        spread = jnp.sum(centred * centred, 1, keepdims=True)
        p1s[step, m] = by_rows((centred * gain).astype(BF16), weights(w))
        put_stat(t1s.at[step, m], mean, spread, gd)
        for copy in l1(step, m):
            copy.start()

    def enter_end(step, m):
        for copy in l1(step, m):
            copy.wait_recv()
        part, mean, spread, gd = join(
            float(cols), p1s[step, m], *get_stat(t1s.at[step, m]),
            p1r[step, m], *get_stat(t1r.at[step, m])
        )
        p2s[step, m] = part.astype(BF16)
        put_stat(t2s.at[step, m], mean, spread, gd)
        if step == OWN:
            p2r[0, m] = part.astype(BF16)
            put_stat(t2r.at[0, m], mean, spread, gd)
        for copy in l2(step, m):
            copy.start()

    def l2_arrival(place, m):
        for i, dst in enumerate((p2r, t2r)):
            move(
                dst.at[place, m], dst.at[place, m], l2send.at[HOP, m, i, place],
                l2recv.at[m, i, place], far,
            ).wait_recv()

    @pl.when(sec == 0)
    def _():
        own_gain_down[...] = gain_times(gain_ref[...], DOWN)

        def enter(m):
            span = to_column(spans[0:1], m * ROWS)
            rows = copies[0, slots[m]].astype(F32) + span * entry[m].astype(F32)
            xs[m] = rows
            enter_begin(OWN, m, rows, gain_ref[...], own_gain_down[...], DOWN)
            enter_end(OWN, m)

        each(enter)

    if_has(NEXT_DOWN, lambda: x_forward(1, NEXT_DOWN))
    x_finish(UP)

    @pl.when(sec > 0)
    def _():
        for p in range(2):
            x_forward(p, PREV_UP)

    @pl.when(sec < last)
    def _():
        x_finish(NEXT_DOWN)
        shard_move(None).wait_recv()
        next_gain_down[...] = gain_times(next_gain[...], NEXT_DOWN)

    def b1(step, m):
        return move(u1s.at[step, m], u1r.at[step, m], b1send.at[step, m], b1recv.at[step, m], mate)

    def b2(step, m):
        places = [(1, far)] if step == OWN else [(0, prev_sec), (1, far_before)]
        return [
            move(
                u2s.at[step, m], u2r.at[place, m], b2send.at[step, m, place],
                b2recv.at[m, place], device,
            )
            for place, device in places
        ]

    def b2_arrival(place, m):
        move(
            u2r.at[place, m], u2r.at[place, m], b2send.at[HOP, m, place],
            b2recv.at[m, place], far,
        ).wait_recv()

    def back_begin(step, m, rows, w):
        u1s[step, m] = by_rows(rows, weights(w))
        b1(step, m).start()

    def back_end(step, m):
        b1(step, m).wait_recv()
        both = (u1s[step, m] + u1r[step, m]).astype(BF16)
        u2s[step, m] = both
        if step == OWN:
            u2r[0, m] = both
        for copy in b2(step, m):
            copy.start()

    def backward(m):
        b2_arrival(1, m)
        grad_act = u2r[0, m].astype(F32) + u2r[1, m].astype(F32)
        pre = pres[m]
        bend = jnp.tanh(CURVE * (pre + 0.044715 * (pre * pre * pre)))
        slope = 0.5 * (1.0 + bend) + 0.5 * pre * (1.0 - bend * bend) * (
            CURVE * (1.0 + 3.0 * 0.044715 * pre * pre)
        )
        dpre = (grad_act * slope).astype(BF16)
        dpre_s[x, m] = dpre
        factor_send(3, m)
        wide = dpre.astype(F32)
        mean_grad = jnp.sum(wide * gsum[...], 1, keepdims=True) / total
        mean_cross = jnp.sum(wide * pre, 1, keepdims=True) / total
        mean, inverse = norm_stat[m, 0], norm_stat[m, 1]
        normed = (xs[m] - mean) * inverse
        dn = times(dpre, weights(DOWN)) * gain_ref[...]
        dx = gs[m] + inverse * (dn - mean_grad - normed * mean_cross)
        gs[m] = dx
        dxb[m] = dx.astype(BF16)

        @pl.when(sec > 0)
        def _():
            y_back(m).start()
            back_begin(HOP, m, dxb[m], PREV_UP)

        peak_src[0:1] += to_lanes(jnp.max(jnp.abs(dx), 1, keepdims=True), m * ROWS)

        @pl.when(sec > 0)
        def _():
            back_end(HOP, m)

    peak_src[...] = jnp.zeros((8, 128), F32)

    @pl.when(sec == last)
    def _():
        def enter(m):
            gs[m] = exit_codes[m].astype(F32) * exit_scale[m]
            gb[x, m] = gs[m].astype(BF16)
            back_begin(OWN, m, gb[x, m], UP)
            factor_send(2, m)
            back_end(OWN, m)

        each(enter)
        x_finish(PREV_UP)

    def forward(m):
        @pl.when(sec > 0)
        def _():
            y_forward(m).wait_recv()
            span = to_column(spans[0:1], m * ROWS)
            xs[m] = copies[0, slots[m]].astype(F32) + span * incf[m].astype(F32)
            l2_arrival(0, m)

        l2_arrival(1, m)
        raw, mean, spread, gd = join(
            float(2 * cols), p2r[0, m].astype(F32), *get_stat(t2r.at[0, m]),
            p2r[1, m].astype(F32), *get_stat(t2r.at[1, m])
        )
        inverse = lax.rsqrt(spread / total + 1e-05)
        pre = raw * inverse
        gsum[...] = gd
        pres[m] = pre
        norm_stat[m, 0] = mean
        norm_stat[m, 1] = inverse
        act = (0.5 * pre * (1.0 + jnp.tanh(CURVE * (pre + 0.044715 * (pre * pre * pre))))).astype(BF16)
        hidden[x, m] = act
        result = xs[m] + times(act, weights(UP))
        span = to_column(spans[1:2], m * ROWS)
        copy_out = copies[1, slots[m]].astype(F32)
        codes = jnp.clip((result - copy_out) / span, -1.0, 1.0).astype(BF16)
        sent[m] = codes

        @pl.when(sec < last)
        def _():
            y_forward(m).start()
            rows = copy_out + span * codes.astype(F32)
            enter_begin(HOP, m, rows, next_gain[...], next_gain_down[...], NEXT_DOWN)

        scaled[x, m] = ((xs[m] - mean) * inverse * gain_ref[...]).astype(BF16)
        factor_send(0, m)
        factor_send(1, m)

        @pl.when(sec < last)
        def _():
            enter_end(HOP, m)

        @pl.when(sec == last)
        def _():
            backward(m)

    each(forward)

    @pl.when(sec < last)
    def _():
        @pl.when(sec > 0)
        def _():
            x_finish(PREV_UP)

        def back(m):
            y_back(m).wait_recv()
            gs[m] = incb[m].astype(F32)
            gb[x, m] = incb[m]
            factor_send(2, m)
            b2_arrival(0, m)
            backward(m)

        each(back)

    quarter = nz // 2
    parity = z % 2

    def unit_pick(side):
        shape = (bot, quarter * unit)
        row = lax.broadcasted_iota(jnp.int32, shape, 0)
        col = lax.broadcasted_iota(jnp.int32, shape, 1)
        source = col + (x * nz + side) * unit
        for k in range(1, quarter):
            source += jnp.where(col >= k * unit, unit, 0)
        return jnp.where(row == source, 1.0, 0.0).astype(BF16)

    def gradient(p, side):
        left, right = (hidden, gb) if p < 2 else (dpre_s, scaled)
        tokens = NX * MICRO * ROWS
        at = slice(p % 2 * half, (p % 2 + 1) * half)
        lhs = times(left[...].reshape(tokens, bot), unit_pick(side)).astype(BF16)
        return by_cols(lhs, right[:, :, :, at].reshape(tokens, half))

    def pair_move(p):
        return move(pair_out.at[p], pair_in.at[p], psend.at[p], precv.at[p], z_mate)

    def gz_move(k):
        slot = (z + 2 * (k + 1)) % nz // 2
        return move(zs.at[slot], rz.at[k], gzsend.at[k], gzrecv.at[k], z_peers[k])

    def piece_rows(p):
        shape = (quarter * 4 * unit, quarter * unit)
        row = lax.broadcasted_iota(jnp.int32, shape, 0)
        col = lax.broadcasted_iota(jnp.int32, shape, 1)
        target = col + p * unit
        for k in range(1, quarter):
            target += jnp.where(col >= k * unit, 3 * unit, 0)
        return jnp.where(row == target, 1.0, 0.0).astype(BF16)

    def gradient_first(pieces):
        for p in pieces:
            pair_out[p] = gradient(p, 1 - parity).astype(BF16)
            pair_move(p).start()
        for p in pieces:
            own[p] = gradient(p, parity)

    def gradient_second():
        rows = 0.0
        for p in range(4):
            pair_move(p).wait_recv()
            both = (own[p] + pair_in[p].astype(F32)).astype(BF16)
            rows += times(piece_rows(p), both)
        zs[...] = rows.astype(BF16).reshape(quarter, 4 * unit, half)
        for k in range(3):
            gz_move(k).start()

    def peak_move(k):
        return move(peak_src, peak_in.at[k], peak_sem.at[0, k], peak_sem.at[1, k], others[k])

    for k in range(3):
        peak_move(k).start()
    factor_wait(0)
    factor_wait(3)
    gradient_first((2, 3))
    factor_wait(1)
    factor_wait(2)
    gradient_first((0, 1))
    gradient_second()

    for k in range(3):
        peak_move(k).wait_recv()
    peak_row = jnp.maximum(
        jnp.maximum(peak_src[0:1], peak_in[0, 0:1]),
        jnp.maximum(peak_in[1, 0:1], peak_in[2, 0:1]),
    )
    peak_row = (peak_row + 1e-05).astype(BF16).astype(F32)

    def codes_back(m):
        returned[m] = (gs[m] / to_column(peak_row, m * ROWS)).astype(BF16)

    each(codes_back)

    result = zs[z // 2].astype(F32)
    for k in range(3):
        gz_move(k).wait_recv()
        result += rz[k].astype(F32)
    own[0] = result
    for p in range(4):
        out = grad_up if p < 2 else grad_down
        out[:, p % 2 * half : (p % 2 + 1) * half] = own[0, p * unit : (p + 1) * unit]

    for k in range(3):
        span_move(k).wait_send()
        peak_move(k).wait_send()

    def drain_micro(m):
        @pl.when(sec == 0)
        def _():
            for copy in l1(OWN, m) + l2(OWN, m):
                copy.wait_send()

        @pl.when(sec == last)
        def _():
            for copy in [b1(OWN, m)] + b2(OWN, m):
                copy.wait_send()

        @pl.when(sec < last)
        def _():
            for copy in l1(HOP, m) + l2(HOP, m) + [y_forward(m)]:
                copy.wait_send()

        @pl.when(sec > 0)
        def _():
            for copy in [b1(HOP, m)] + b2(HOP, m) + [y_back(m)]:
                copy.wait_send()

    each(drain_micro)

    @pl.when(sec > 0)
    def _():
        shard_move(NEXT_DOWN).wait_send()
        shard_move(None).wait_send()

    @pl.when(sec < last)
    def _():
        shard_move(PREV_UP).wait_send()

    for m in ALL:
        def drain_x():
            for p in range(2):
                for kind in range(4):
                    x_move(p, m, kind).wait_send()

        if_has(m, drain_x)

    for p in range(4):
        pair_move(p).wait_send()
    for k in range(3):
        gz_move(k).wait_send()

    def drain_factors(m):
        for which in range(4):
            for k in range(3):
                factor_move(which, m, k).wait_send()

    each(drain_factors)

    def drain_z(slot, carry):
        for m in ALL:
            def drain():
                @pl.when((z < nz - 1) & (slot <= z))
                def _():
                    z_move(0, slot, m).wait_send()

                @pl.when((z > 0) & (slot >= z))
                def _():
                    z_move(1, slot, m).wait_send()

            if_has(m, drain)

        return carry

    lax.fori_loop(0, nz, drain_z, 0)


def solution(mesh):
    nz = mesh.shape["dp"] // NX

    def local(stored, entry, exit_codes, exit_scales, slot_ids, gain, down, up):
        unit, cols = down.shape[1], down.shape[2]
        bot = unit * mesh.shape["dp"]
        tokens = MICRO * ROWS
        pad = lambda w: jnp.pad(w, ((0, PAD - unit), (0, 0)))
        shard = jnp.stack([pad(down[0]), pad(up[0])])
        block = (MICRO, ROWS, cols)
        small = (MICRO, ROWS, bot)
        stat = (2, MICRO, 8, 128)
        dma = pltpu.SemaphoreType.DMA
        vm = pltpu.VMEM
        xrows = bot // NX
        scratch = [
            vm((nz, 4, PAD, cols), BF16),
            vm((4, NX, 2, xrows // 2, cols), BF16),
            vm((8, 128), F32), vm((3, 8, 128), F32), vm((8, 128), F32),
            vm(block, BF16), vm(block, BF16),
            vm(block, F32),
            vm((MICRO, 2, ROWS, 1), F32),
            vm(small, F32),
            vm((1, bot), F32), vm((1, bot), F32), vm((1, bot), F32), vm((1, cols), F32),
            vm((2, *small), F32), vm((2, *small), F32), vm(stat, F32), vm(stat, F32),
            vm((2, *small), BF16), vm((2, *small), BF16), vm(stat, F32), vm(stat, F32),
            vm((2, *small), F32), vm((2, *small), F32),
            vm((2, *small), BF16), vm((2, *small), BF16),
            vm(block, F32), vm(block, BF16),
            vm((8, 128), F32), vm((3, 8, 128), F32),
            vm((NX, *block), BF16), vm((NX, *small), BF16),
            vm((NX, *block), BF16), vm((NX, *small), BF16),
            vm((4, xrows // 2, cols // 2), BF16), vm((4, xrows // 2, cols // 2), BF16),
            vm((4, xrows // 2, cols // 2), F32),
            vm((nz // 2, 4 * unit, cols // 2), BF16),
            vm((3, 4 * unit, cols // 2), BF16),
            dma((2, 3)),
            dma((3,)), dma((3,)),
            dma((2, nz, 4)), dma((nz, 4)),
            dma((2, 4, 4)), dma((2, 4, 4)),
            dma((2, MICRO, 2)), dma((2, MICRO, 2)), dma((2, MICRO, 2, 2)), dma((MICRO, 2, 2)),
            dma((2, MICRO)), dma((2, MICRO)), dma((2, MICRO, 2)), dma((MICRO, 2)),
            dma((MICRO,)), dma((MICRO,)), dma((MICRO,)), dma((MICRO,)),
            dma((2, 3)),
            dma((4, MICRO, 3)), dma((4, MICRO, 3)),
            dma((4,)), dma((4,)),
            dma((3,)), dma((3,)),
        ]
        in_vmem = pl.BlockSpec(memory_space=pltpu.VMEM)
        sent, returned, grad_down, grad_up = pl.pallas_call(
            lambda *refs: relay_kernel(nz, *refs),
            out_shape=(
                jax.ShapeDtypeStruct(block, BF16),
                jax.ShapeDtypeStruct(block, BF16),
                jax.ShapeDtypeStruct((unit, cols), F32),
                jax.ShapeDtypeStruct((unit, cols), F32),
            ),
            in_specs=[in_vmem] * 4 + [pl.BlockSpec(memory_space=pltpu.SMEM)] + [in_vmem] * 2,
            out_specs=(in_vmem,) * 4,
            scratch_shapes=scratch,
            compiler_params=pltpu.CompilerParams(
                collective_id=0, has_side_effects=True, vmem_limit_bytes=48 * 2**20
            ),
        )(
            stored[0].reshape(2, MICRO, ROWS, cols),
            entry.reshape(block),
            exit_codes.reshape(block),
            exit_scales.reshape(MICRO, ROWS, 1),
            slot_ids[0],
            gain,
            shard,
        )
        return (
            sent.reshape(1, tokens, cols),
            returned.reshape(1, tokens, cols),
            grad_down[None],
            grad_up[None],
        )

    in_specs = (
        P("section", None, "dp", "tensor"),
        P("dp", "tensor"),
        P("dp", "tensor"),
        P("dp"),
        P("dp", None),
        P("section", "tensor"),
        P("section", "dp", "tensor"),
        P("section", "dp", "tensor"),
    )
    out_specs = (P("section", "dp", "tensor"),) * 4
    return jax.shard_map(local, mesh=mesh, in_specs=in_specs, out_specs=out_specs, check_vma=False)
```

```python
import math

import jax
import jax.numpy as jnp
from jax import lax
from jax.experimental import pallas as pl
from jax.experimental.pallas import tpu as pltpu
from jax.sharding import PartitionSpec as P

MESH = pl.DeviceIdType.MESH
F32 = jnp.float32
BF16 = jnp.bfloat16
MICRO = 4
ROWS = 32
NX = 4
PAD = 16
DOWN, UP, NEXT_DOWN, PREV_UP = ALL = (0, 1, 2, 3)
OWN, HOP = 0, 1
CURVE = math.sqrt(2.0 / math.pi)


def by_rows(left, right):
    return lax.dot_general(left, right, (((1,), (1,)), ((), ())), preferred_element_type=F32)


def by_cols(left, right):
    return lax.dot_general(left, right, (((0,), (0,)), ((), ())), preferred_element_type=F32)


def times(left, right):
    return jnp.dot(left, right, preferred_element_type=F32)


def lane_mask(shift):
    row = lax.broadcasted_iota(jnp.int32, (ROWS, 128), 0)
    lane = lax.broadcasted_iota(jnp.int32, (ROWS, 128), 1)
    return lane == row + shift


def to_lanes(column, shift):
    return jnp.sum(jnp.where(lane_mask(shift), column, 0.0), 0, keepdims=True)


def to_column(lanes, shift):
    return jnp.sum(jnp.where(lane_mask(shift), lanes, 0.0), 1, keepdims=True)


def shard_rows(shards, unit, part):
    shape = (shards * unit, shards * PAD)
    row = lax.broadcasted_iota(jnp.int32, shape, 0)
    col = lax.broadcasted_iota(jnp.int32, shape, 1)
    hit = row < 0
    for k in range(shards):
        for i in range(unit if part is None else unit // 3):
            if part is None:
                hit |= (row == k * unit + i) & (col == k * PAD + i)
            else:
                hit |= (row == k * unit + 3 * i + part) & (col == k * PAD + unit + i)
    return jnp.where(hit, 1.0, 0.0).astype(BF16)


def relay_kernel(
    nz, copies, entry, exit_codes, exit_scale, slots, gain_ref, shard,
    sent, returned, grad_down, grad_up,
    zbuf, wv, span_src, span_in, spans, incf, incb, xs, norm_stat, pres, gsum,
    own_gain_down, next_gain_down, next_gain,
    p1s, p1r, t1s, t1r, p2s, p2r, t2s, t2r, u1s, u1r, u2s, u2r,
    gs, dxb, peak_src, peak_in, scaled, hidden, gb, dpre_s, pair_out, pair_in, own, zs, rz,
    span_sem, ssend, srecv, zsend, zrecv, xsend, xrecv, l1send, l1recv, l2send, l2recv,
    b1send, b1recv, b2send, b2recv, ysend, yrecv, wsend, wrecv, peak_sem,
    fsend, frecv, rsend, rrecv, psend, precv, gzsend, gzrecv,
):
    sec = lax.axis_index("section")
    last = lax.axis_size("section") - 1
    dp = lax.axis_index("dp")
    ten = lax.axis_index("tensor")
    x = dp // nz
    z = dp % nz
    half_z = nz // 2
    unit = grad_down.shape[0]
    cols = gain_ref.shape[1]
    half = cols // 2
    pack = shard.shape[2]
    bot = pres.shape[2]
    total = cols * 4
    xr, xl, xo = (x + 1) % NX, (x + NX - 1) % NX, (x + 2) % NX
    to_right = {"dp": xr * nz + z}
    to_left = {"dp": xl * nz + z}
    mate = {"tensor": ten + 1 - 2 * (ten % 2)}
    far = {"tensor": (ten + 2) % 4}
    others = [{"tensor": (ten + k) % 4} for k in (1, 2, 3)]
    next_sec = {"section": (sec + 1) % (last + 1)}
    prev_sec = {"section": (sec + last) % (last + 1)}
    z_up = {"dp": x * nz + (z + 1) % nz}
    z_down = {"dp": x * nz + (z + nz - 1) % nz}

    barrier = pltpu.get_barrier_semaphore()
    x_peers = [{"dp": (x + k) % NX * nz + z} for k in (1, 2, 3)]
    z_peers = [{"dp": x * nz + (z + 2 * k) % nz} for k in (1, 2, 3)]
    z_mate = {"dp": dp + 1 - 2 * (z % 2)}
    diagonal = [{"section": to["section"], "tensor": far["tensor"]} for to in (next_sec, prev_sec)]
    friends = others + [next_sec, prev_sec, z_up, z_down] + x_peers + z_peers + diagonal
    for friend in friends:
        pl.semaphore_signal(barrier, inc=1, device_id=friend, device_id_type=MESH)
    pl.semaphore_wait(barrier, len(friends))

    def move(src, dst, send, recv, device):
        return pltpu.make_async_remote_copy(
            src_ref=src, dst_ref=dst, send_sem=send, recv_sem=recv,
            device_id=device, device_id_type=MESH,
        )

    def each(step):
        def tick(m, carry):
            step(m)
            return carry

        lax.fori_loop(0, MICRO, tick, 0)

    has = {DOWN: None, UP: None, NEXT_DOWN: sec < last, PREV_UP: sec > 0}

    def if_has(m, step):
        if has[m] is None:
            step()
        else:
            pl.when(has[m])(step)

    def shard_move(m):
        if m == NEXT_DOWN:
            return move(shard.at[DOWN], zbuf.at[z, m], ssend.at[0], srecv.at[0], prev_sec)
        if m == PREV_UP:
            return move(shard.at[UP], zbuf.at[z, m], ssend.at[1], srecv.at[1], next_sec)
        return move(gain_ref, next_gain, ssend.at[2], srecv.at[2], prev_sec)

    def z_move(way, slot, m):
        return move(
            zbuf.at[slot, m], zbuf.at[slot, m], zsend.at[way, slot, m], zrecv.at[slot, m],
            z_up if way == 0 else z_down,
        )

    def z_begin(m):
        @pl.when(z < nz - 1)
        def _():
            z_move(0, z, m).start()

        @pl.when(z > 0)
        def _():
            z_move(1, z, m).start()

    def z_step(k):
        for m in ALL:
            def pass_on():
                @pl.when(z - k >= 0)
                def _():
                    z_move(0, z - k, m).wait_recv()

                    @pl.when(z < nz - 1)
                    def _():
                        z_move(0, z - k, m).start()

                @pl.when(z + k < nz)
                def _():
                    z_move(1, z + k, m).wait_recv()

                    @pl.when(z > 0)
                    def _():
                        z_move(1, z + k, m).start()

            if_has(m, pass_on)

    def z_steps(first, end):
        def step(k, carry):
            z_step(k)
            return carry

        lax.fori_loop(first, end, step, 0)

    group = [z // half_z, 1 - z // half_z]

    def x_move(p, m, kind):
        g = group[p]
        block, device, part = {
            0: (x, to_right, slice(None)),
            1: (x, to_left, slice(None)),
            2: (xl, to_right, slice(0, half)),
            3: (xr, to_left, slice(half, cols)),
        }[kind]
        ref = wv.at[m, block, g] if kind < 2 else wv.at[m, block, g, :, part]
        return move(ref, ref, xsend.at[p, m, kind], xrecv.at[p, m, kind], device)

    def x_arrival(p, m, kind):
        g = group[p]
        ref = {
            0: lambda: wv.at[m, xl, g],
            1: lambda: wv.at[m, xr, g],
            2: lambda: wv.at[m, xo, g, :, slice(0, half)],
            3: lambda: wv.at[m, xo, g, :, slice(half, cols)],
        }[kind]()
        move(ref, ref, xsend.at[p, m, kind], xrecv.at[p, m, kind], to_right).wait_recv()

    def x_own(p, m):
        g = group[p]
        block = zbuf[pl.ds(g * half_z, half_z), m].reshape(half_z * PAD, pack)
        wv[m, x, g, :, 0:pack] = times(shard_rows(half_z, unit, None), block).astype(BF16)
        tail = 0.0
        for j in range(3):
            tail += times(
                shard_rows(half_z, unit, j), block[:, j * (cols - pack) : (j + 1) * (cols - pack)]
            )
        wv[m, x, g, :, pack:cols] = tail.astype(BF16)
        x_move(p, m, 0).start()
        x_move(p, m, 1).start()

    def x_forward(p, m):
        x_arrival(p, m, 0)
        x_move(p, m, 2).start()
        x_arrival(p, m, 1)
        x_move(p, m, 3).start()

    def x_finish(m):
        for p in range(2):
            x_arrival(p, m, 2)
            x_arrival(p, m, 3)

    @pl.when(sec > 0)
    def _():
        shard_move(NEXT_DOWN).start()
        shard_move(None).start()

    @pl.when(sec < last)
    def _():
        shard_move(PREV_UP).start()

    for m in (DOWN, UP):
        zbuf[z, m] = shard[m]
        z_begin(m)

    def squares(m, carry):
        sums = []
        for k in range(2):
            rows = copies[k, slots[m]].astype(F32)
            sums.append(to_lanes(jnp.sum(rows * rows, 1, keepdims=True), m * ROWS))
        return carry[0] + sums[0], carry[1] + sums[1]

    nothing = jnp.zeros((1, 128), F32)
    square_in, square_out = lax.fori_loop(0, MICRO, squares, (nothing, nothing))
    span_src[...] = jnp.zeros((8, 128), F32)
    span_src[0:1] = square_in
    span_src[1:2] = square_out

    def span_move(k):
        return move(span_src, span_in.at[k], span_sem.at[0, k], span_sem.at[1, k], others[k])

    for k in range(3):
        span_move(k).start()

    @pl.when(sec < last)
    def _():
        shard_move(NEXT_DOWN).wait_recv()
        z_begin(NEXT_DOWN)

    @pl.when(sec > 0)
    def _():
        shard_move(PREV_UP).wait_recv()
        z_begin(PREV_UP)

    z_steps(1, half_z)
    for m in (DOWN, UP, NEXT_DOWN):
        if_has(m, lambda: x_own(0, m))
    z_steps(half_z, half_z + 2)
    x_forward(0, DOWN)
    z_steps(half_z + 2, half_z + 3)
    x_forward(0, UP)
    z_steps(half_z + 3, nz)
    x_own(1, DOWN)
    x_own(1, UP)
    if_has(NEXT_DOWN, lambda: x_forward(0, NEXT_DOWN))
    for k in range(3):
        span_move(k).wait_recv()
    spans[...] = 2.0 * jnp.sqrt(
        (span_src[...] + span_in[0] + span_in[1] + span_in[2]) / total + 1e-05
    )
    x_forward(1, DOWN)
    if_has(NEXT_DOWN, lambda: x_own(1, NEXT_DOWN))
    x_forward(1, UP)
    x_finish(DOWN)
    for p in range(2):
        if_has(PREV_UP, lambda: x_own(p, PREV_UP))

    def weights(m):
        return wv[m].reshape(bot, cols)

    def gain_times(gain, m):
        first = gain.astype(BF16).astype(F32)
        second = (gain - first).astype(BF16).astype(F32)
        third = gain - first - second
        row = lax.broadcasted_iota(jnp.int32, (PAD, cols), 0)
        terms = jnp.where(
            row == 0, first, jnp.where(row == 1, second, jnp.where(row == 2, third, 0.0))
        ).astype(BF16)
        return jnp.sum(by_rows(terms, weights(m)), 0, keepdims=True)

    pieces = bot // 128

    def put_stat(ref, mean, spread, gd):
        ref[...] = jnp.zeros((8, 128), F32)
        ref[0:1] = to_lanes(mean, 0)
        ref[1:2] = to_lanes(spread, 0)
        for i in range(pieces):
            ref[2 + i : 3 + i] = gd[:, i * 128 : (i + 1) * 128]

    def get_stat(ref):
        gd = jnp.concatenate([ref[2 + i : 3 + i] for i in range(pieces)], axis=1)
        return to_column(ref[0:1], 0), to_column(ref[1:2], 0), gd

    def join(count, p, mean, spread, gd, p_other, mean_other, spread_other, gd_other):
        both = 0.5 * (mean + mean_other)
        mine, theirs = mean - both, mean_other - both
        spread_both = spread + spread_other + count * (mine * mine + theirs * theirs)
        p_both = (p + p_other) + (mine * gd + theirs * gd_other)
        return p_both, both, spread_both, gd + gd_other

    far_of, far_before = diagonal

    def l1(step, m):
        return [
            move(src.at[step, m], dst.at[step, m], l1send.at[step, m, i], l1recv.at[step, m, i], mate)
            for i, (src, dst) in enumerate(((p1s, p1r), (t1s, t1r)))
        ]

    def l2(step, m):
        places = [(1, far)] if step == OWN else [(0, next_sec), (1, far_of)]
        return [
            move(
                src.at[step, m], dst.at[place, m], l2send.at[step, m, i, place],
                l2recv.at[m, i, place], device,
            )
            for i, (src, dst) in enumerate(((p2s, p2r), (t2s, t2r)))
            for place, device in places
        ]

    def y_forward(m):
        return move(sent.at[m], incf.at[m], ysend.at[m], yrecv.at[m], next_sec)

    def y_back(m):
        return move(dxb.at[m], incb.at[m], wsend.at[m], wrecv.at[m], prev_sec)

    factors = (hidden, dpre_s)

    def factor_move(which, m, k):
        ref = factors[which].at[x, m]
        return move(ref, ref, fsend.at[which, m, k], frecv.at[which, m, k], x_peers[k])

    def factor_send(which, m):
        for k in range(3):
            factor_move(which, m, k).start()

    def factor_wait(which):
        def wait(m):
            for k in range(3):
                ref = factors[which].at[(x + NX - 1 - k) % NX, m]
                move(ref, ref, fsend.at[which, m, k], frecv.at[which, m, k], x_peers[k]).wait_recv()

        each(wait)

    ring_rows = (scaled, gb)

    def ring_move(which, m, kind):
        block, device, part = {
            0: (x, to_right, slice(None)),
            1: (x, to_left, slice(None)),
            2: (xl, to_right, slice(0, half)),
            3: (xr, to_left, slice(half, cols)),
        }[kind]
        rows = ring_rows[which]
        ref = rows.at[block, m] if kind < 2 else rows.at[block, m, :, part]
        return move(ref, ref, rsend.at[which, m, kind], rrecv.at[which, m, kind], device)

    def ring_arrival(which, m, kind):
        rows = ring_rows[which]
        ref = {
            0: lambda: rows.at[xl, m],
            1: lambda: rows.at[xr, m],
            2: lambda: rows.at[xo, m, :, slice(0, half)],
            3: lambda: rows.at[xo, m, :, slice(half, cols)],
        }[kind]()
        move(ref, ref, rsend.at[which, m, kind], rrecv.at[which, m, kind], to_right).wait_recv()

    def ring_send(which, m):
        ring_move(which, m, 0).start()
        ring_move(which, m, 1).start()

    def ring_forward(which):
        def step(m):
            ring_arrival(which, m, 0)
            ring_move(which, m, 2).start()
            ring_arrival(which, m, 1)
            ring_move(which, m, 3).start()

        each(step)

    def ring_end(which):
        def step(m):
            ring_arrival(which, m, 2)
            ring_arrival(which, m, 3)

        each(step)

    def enter_begin(step, m, rows, gain, gd, w):
        mean = jnp.sum(rows, 1, keepdims=True) / cols
        centred = rows - mean
        spread = jnp.sum(centred * centred, 1, keepdims=True)
        p1s[step, m] = by_rows((centred * gain).astype(BF16), weights(w))
        put_stat(t1s.at[step, m], mean, spread, gd)
        for copy in l1(step, m):
            copy.start()

    def enter_end(step, m):
        for copy in l1(step, m):
            copy.wait_recv()
        part, mean, spread, gd = join(
            float(cols), p1s[step, m], *get_stat(t1s.at[step, m]),
            p1r[step, m], *get_stat(t1r.at[step, m])
        )
        p2s[step, m] = part.astype(BF16)
        put_stat(t2s.at[step, m], mean, spread, gd)
        if step == OWN:
            p2r[0, m] = part.astype(BF16)
            put_stat(t2r.at[0, m], mean, spread, gd)
        for copy in l2(step, m):
            copy.start()

    def l2_arrival(place, m):
        for i, dst in enumerate((p2r, t2r)):
            move(
                dst.at[place, m], dst.at[place, m], l2send.at[HOP, m, i, place],
                l2recv.at[m, i, place], far,
            ).wait_recv()

    @pl.when(sec == 0)
    def _():
        own_gain_down[...] = gain_times(gain_ref[...], DOWN)

        def enter(m):
            span = to_column(spans[0:1], m * ROWS)
            rows = copies[0, slots[m]].astype(F32) + span * entry[m].astype(F32)
            xs[m] = rows
            enter_begin(OWN, m, rows, gain_ref[...], own_gain_down[...], DOWN)
            enter_end(OWN, m)

        each(enter)

    if_has(NEXT_DOWN, lambda: x_forward(1, NEXT_DOWN))
    x_finish(UP)

    @pl.when(sec > 0)
    def _():
        for p in range(2):
            x_forward(p, PREV_UP)

    @pl.when(sec < last)
    def _():
        x_finish(NEXT_DOWN)
        shard_move(None).wait_recv()
        next_gain_down[...] = gain_times(next_gain[...], NEXT_DOWN)

    def b1(step, m):
        return move(u1s.at[step, m], u1r.at[step, m], b1send.at[step, m], b1recv.at[step, m], mate)

    def b2(step, m):
        places = [(1, far)] if step == OWN else [(0, prev_sec), (1, far_before)]
        return [
            move(
                u2s.at[step, m], u2r.at[place, m], b2send.at[step, m, place],
                b2recv.at[m, place], device,
            )
            for place, device in places
        ]

    def b2_arrival(place, m):
        move(
            u2r.at[place, m], u2r.at[place, m], b2send.at[HOP, m, place],
            b2recv.at[m, place], far,
        ).wait_recv()

    def back_begin(step, m, rows, w):
        u1s[step, m] = by_rows(rows, weights(w))
        b1(step, m).start()

    def back_end(step, m):
        b1(step, m).wait_recv()
        both = (u1s[step, m] + u1r[step, m]).astype(BF16)
        u2s[step, m] = both
        if step == OWN:
            u2r[0, m] = both
        for copy in b2(step, m):
            copy.start()

    def backward(m):
        b2_arrival(1, m)
        grad_act = u2r[0, m].astype(F32) + u2r[1, m].astype(F32)
        pre = pres[m]
        bend = jnp.tanh(CURVE * (pre + 0.044715 * (pre * pre * pre)))
        slope = 0.5 * (1.0 + bend) + 0.5 * pre * (1.0 - bend * bend) * (
            CURVE * (1.0 + 3.0 * 0.044715 * pre * pre)
        )
        dpre = (grad_act * slope).astype(BF16)
        dpre_s[x, m] = dpre
        factor_send(1, m)
        wide = dpre.astype(F32)
        mean_grad = jnp.sum(wide * gsum[...], 1, keepdims=True) / total
        mean_cross = jnp.sum(wide * pre, 1, keepdims=True) / total
        mean, inverse = norm_stat[m, 0], norm_stat[m, 1]
        normed = (xs[m] - mean) * inverse
        dn = times(dpre, weights(DOWN)) * gain_ref[...]
        dx = gs[m] + inverse * (dn - mean_grad - normed * mean_cross)
        gs[m] = dx
        dxb[m] = dx.astype(BF16)

        @pl.when(sec > 0)
        def _():
            y_back(m).start()
            back_begin(HOP, m, dxb[m], PREV_UP)

        peak_src[0:1] += to_lanes(jnp.max(jnp.abs(dx), 1, keepdims=True), m * ROWS)

        @pl.when(sec > 0)
        def _():
            back_end(HOP, m)

    peak_src[...] = jnp.zeros((8, 128), F32)

    @pl.when(sec == last)
    def _():
        def enter(m):
            gs[m] = exit_codes[m].astype(F32) * exit_scale[m]
            gb[x, m] = gs[m].astype(BF16)
            back_begin(OWN, m, gb[x, m], UP)
            ring_send(1, m)
            back_end(OWN, m)

        each(enter)
        x_finish(PREV_UP)

    def forward(m):
        @pl.when(sec > 0)
        def _():
            y_forward(m).wait_recv()
            span = to_column(spans[0:1], m * ROWS)
            xs[m] = copies[0, slots[m]].astype(F32) + span * incf[m].astype(F32)
            l2_arrival(0, m)

        l2_arrival(1, m)
        raw, mean, spread, gd = join(
            float(2 * cols), p2r[0, m].astype(F32), *get_stat(t2r.at[0, m]),
            p2r[1, m].astype(F32), *get_stat(t2r.at[1, m])
        )
        inverse = lax.rsqrt(spread / total + 1e-05)
        pre = raw * inverse
        gsum[...] = gd
        pres[m] = pre
        norm_stat[m, 0] = mean
        norm_stat[m, 1] = inverse
        act = (0.5 * pre * (1.0 + jnp.tanh(CURVE * (pre + 0.044715 * (pre * pre * pre))))).astype(BF16)
        hidden[x, m] = act
        result = xs[m] + times(act, weights(UP))
        span = to_column(spans[1:2], m * ROWS)
        copy_out = copies[1, slots[m]].astype(F32)
        codes = jnp.clip((result - copy_out) / span, -1.0, 1.0).astype(BF16)
        sent[m] = codes

        @pl.when(sec < last)
        def _():
            y_forward(m).start()
            rows = copy_out + span * codes.astype(F32)
            enter_begin(HOP, m, rows, next_gain[...], next_gain_down[...], NEXT_DOWN)

        scaled[x, m] = ((xs[m] - mean) * inverse * gain_ref[...]).astype(BF16)
        ring_send(0, m)
        factor_send(0, m)

        @pl.when(sec < last)
        def _():
            enter_end(HOP, m)

        @pl.when(sec == last)
        def _():
            backward(m)

    each(forward)
    ring_forward(0)

    @pl.when(sec < last)
    def _():
        @pl.when(sec > 0)
        def _():
            x_finish(PREV_UP)

        def back(m):
            y_back(m).wait_recv()
            gs[m] = incb[m].astype(F32)
            gb[x, m] = incb[m]
            ring_send(1, m)
            b2_arrival(0, m)
            backward(m)

        each(back)

    ring_forward(1)

    quarter = nz // 2
    parity = z % 2

    def unit_pick(side):
        shape = (bot, quarter * unit)
        row = lax.broadcasted_iota(jnp.int32, shape, 0)
        col = lax.broadcasted_iota(jnp.int32, shape, 1)
        source = col + (x * nz + side) * unit
        for k in range(1, quarter):
            source += jnp.where(col >= k * unit, unit, 0)
        return jnp.where(row == source, 1.0, 0.0).astype(BF16)

    def gradient(p, side):
        left, right = (hidden, gb) if p < 2 else (dpre_s, scaled)
        tokens = NX * MICRO * ROWS
        at = slice(p % 2 * half, (p % 2 + 1) * half)
        lhs = times(left[...].reshape(tokens, bot), unit_pick(side)).astype(BF16)
        return by_cols(lhs, right[:, :, :, at].reshape(tokens, half))

    def pair_move(p):
        return move(pair_out.at[p], pair_in.at[p], psend.at[p], precv.at[p], z_mate)

    def gz_move(k):
        slot = (z + 2 * (k + 1)) % nz // 2
        return move(zs.at[slot], rz.at[k], gzsend.at[k], gzrecv.at[k], z_peers[k])

    def piece_rows(p):
        shape = (quarter * 4 * unit, quarter * unit)
        row = lax.broadcasted_iota(jnp.int32, shape, 0)
        col = lax.broadcasted_iota(jnp.int32, shape, 1)
        target = col + p * unit
        for k in range(1, quarter):
            target += jnp.where(col >= k * unit, 3 * unit, 0)
        return jnp.where(row == target, 1.0, 0.0).astype(BF16)

    def gradient_first(pieces):
        for p in pieces:
            pair_out[p] = gradient(p, 1 - parity).astype(BF16)
            pair_move(p).start()
        for p in pieces:
            own[p] = gradient(p, parity)

    def gradient_second():
        rows = 0.0
        for p in range(4):
            pair_move(p).wait_recv()
            both = (own[p] + pair_in[p].astype(F32)).astype(BF16)
            rows += times(piece_rows(p), both)
        zs[...] = rows.astype(BF16).reshape(quarter, 4 * unit, half)
        for k in range(3):
            gz_move(k).start()

    def peak_move(k):
        return move(peak_src, peak_in.at[k], peak_sem.at[0, k], peak_sem.at[1, k], others[k])

    for k in range(3):
        peak_move(k).start()
    ring_end(0)
    factor_wait(1)
    gradient_first((2, 3))
    factor_wait(0)
    ring_end(1)
    gradient_first((0, 1))
    gradient_second()

    for k in range(3):
        peak_move(k).wait_recv()
    peak_row = jnp.maximum(
        jnp.maximum(peak_src[0:1], peak_in[0, 0:1]),
        jnp.maximum(peak_in[1, 0:1], peak_in[2, 0:1]),
    )
    peak_row = (peak_row + 1e-05).astype(BF16).astype(F32)

    def codes_back(m):
        returned[m] = (gs[m] / to_column(peak_row, m * ROWS)).astype(BF16)

    each(codes_back)

    result = zs[z // 2].astype(F32)
    for k in range(3):
        gz_move(k).wait_recv()
        result += rz[k].astype(F32)
    own[0] = result
    for p in range(4):
        out = grad_up if p < 2 else grad_down
        out[:, p % 2 * half : (p % 2 + 1) * half] = own[0, p * unit : (p + 1) * unit]

    for k in range(3):
        span_move(k).wait_send()
        peak_move(k).wait_send()

    def drain_micro(m):
        @pl.when(sec == 0)
        def _():
            for copy in l1(OWN, m) + l2(OWN, m):
                copy.wait_send()

        @pl.when(sec == last)
        def _():
            for copy in [b1(OWN, m)] + b2(OWN, m):
                copy.wait_send()

        @pl.when(sec < last)
        def _():
            for copy in l1(HOP, m) + l2(HOP, m) + [y_forward(m)]:
                copy.wait_send()

        @pl.when(sec > 0)
        def _():
            for copy in [b1(HOP, m)] + b2(HOP, m) + [y_back(m)]:
                copy.wait_send()

    each(drain_micro)

    @pl.when(sec > 0)
    def _():
        shard_move(NEXT_DOWN).wait_send()
        shard_move(None).wait_send()

    @pl.when(sec < last)
    def _():
        shard_move(PREV_UP).wait_send()

    for m in ALL:
        def drain_x():
            for p in range(2):
                for kind in range(4):
                    x_move(p, m, kind).wait_send()

        if_has(m, drain_x)

    for p in range(4):
        pair_move(p).wait_send()
    for k in range(3):
        gz_move(k).wait_send()

    def drain_factors(m):
        for which in range(2):
            for k in range(3):
                factor_move(which, m, k).wait_send()
        for which in range(2):
            for kind in range(4):
                ring_move(which, m, kind).wait_send()

    each(drain_factors)

    def drain_z(slot, carry):
        for m in ALL:
            def drain():
                @pl.when((z < nz - 1) & (slot <= z))
                def _():
                    z_move(0, slot, m).wait_send()

                @pl.when((z > 0) & (slot >= z))
                def _():
                    z_move(1, slot, m).wait_send()

            if_has(m, drain)

        return carry

    lax.fori_loop(0, nz, drain_z, 0)


def solution(mesh):
    nz = mesh.shape["dp"] // NX

    def local(stored, entry, exit_codes, exit_scales, slot_ids, gain, down, up):
        unit, cols = down.shape[1], down.shape[2]
        bot = unit * mesh.shape["dp"]
        tokens = MICRO * ROWS
        pack = cols * unit // PAD // 128 * 128 + 128

        def packed(w):
            tail = w[:, pack:].reshape(PAD - unit, unit // (PAD - unit) * (cols - pack))
            tail = jnp.pad(tail, ((0, 0), (0, pack - tail.shape[1])))
            return jnp.concatenate([w[:, :pack], tail])

        shard = jnp.stack([packed(down[0]), packed(up[0])])
        block = (MICRO, ROWS, cols)
        small = (MICRO, ROWS, bot)
        stat = (2, MICRO, 8, 128)
        dma = pltpu.SemaphoreType.DMA
        vm = pltpu.VMEM
        xrows = bot // NX
        scratch = [
            vm((nz, 4, PAD, pack), BF16),
            vm((4, NX, 2, xrows // 2, cols), BF16),
            vm((8, 128), F32), vm((3, 8, 128), F32), vm((8, 128), F32),
            vm(block, BF16), vm(block, BF16),
            vm(block, F32),
            vm((MICRO, 2, ROWS, 1), F32),
            vm(small, F32),
            vm((1, bot), F32), vm((1, bot), F32), vm((1, bot), F32), vm((1, cols), F32),
            vm((2, *small), F32), vm((2, *small), F32), vm(stat, F32), vm(stat, F32),
            vm((2, *small), BF16), vm((2, *small), BF16), vm(stat, F32), vm(stat, F32),
            vm((2, *small), F32), vm((2, *small), F32),
            vm((2, *small), BF16), vm((2, *small), BF16),
            vm(block, F32), vm(block, BF16),
            vm((8, 128), F32), vm((3, 8, 128), F32),
            vm((NX, *block), BF16), vm((NX, *small), BF16),
            vm((NX, *block), BF16), vm((NX, *small), BF16),
            vm((4, xrows // 2, cols // 2), BF16), vm((4, xrows // 2, cols // 2), BF16),
            vm((4, xrows // 2, cols // 2), F32),
            vm((nz // 2, 4 * unit, cols // 2), BF16),
            vm((3, 4 * unit, cols // 2), BF16),
            dma((2, 3)),
            dma((3,)), dma((3,)),
            dma((2, nz, 4)), dma((nz, 4)),
            dma((2, 4, 4)), dma((2, 4, 4)),
            dma((2, MICRO, 2)), dma((2, MICRO, 2)), dma((2, MICRO, 2, 2)), dma((MICRO, 2, 2)),
            dma((2, MICRO)), dma((2, MICRO)), dma((2, MICRO, 2)), dma((MICRO, 2)),
            dma((MICRO,)), dma((MICRO,)), dma((MICRO,)), dma((MICRO,)),
            dma((2, 3)),
            dma((2, MICRO, 3)), dma((2, MICRO, 3)),
            dma((2, MICRO, 4)), dma((2, MICRO, 4)),
            dma((4,)), dma((4,)),
            dma((3,)), dma((3,)),
        ]
        in_vmem = pl.BlockSpec(memory_space=pltpu.VMEM)
        sent, returned, grad_down, grad_up = pl.pallas_call(
            lambda *refs: relay_kernel(nz, *refs),
            out_shape=(
                jax.ShapeDtypeStruct(block, BF16),
                jax.ShapeDtypeStruct(block, BF16),
                jax.ShapeDtypeStruct((unit, cols), F32),
                jax.ShapeDtypeStruct((unit, cols), F32),
            ),
            in_specs=[in_vmem] * 4 + [pl.BlockSpec(memory_space=pltpu.SMEM)] + [in_vmem] * 2,
            out_specs=(in_vmem,) * 4,
            scratch_shapes=scratch,
            compiler_params=pltpu.CompilerParams(
                collective_id=0, has_side_effects=True, vmem_limit_bytes=48 * 2**20
            ),
        )(
            stored[0].reshape(2, MICRO, ROWS, cols),
            entry.reshape(block),
            exit_codes.reshape(block),
            exit_scales.reshape(MICRO, ROWS, 1),
            slot_ids[0],
            gain,
            shard,
        )
        return (
            sent.reshape(1, tokens, cols),
            returned.reshape(1, tokens, cols),
            grad_down[None],
            grad_up[None],
        )

    in_specs = (
        P("section", None, "dp", "tensor"),
        P("dp", "tensor"),
        P("dp", "tensor"),
        P("dp"),
        P("dp", None),
        P("section", "tensor"),
        P("section", "dp", "tensor"),
        P("section", "dp", "tensor"),
    )
    out_specs = (P("section", "dp", "tensor"),) * 4
    return jax.shard_map(local, mesh=mesh, in_specs=in_specs, out_specs=out_specs, check_vma=False)
```

```python
import math

import jax
import jax.numpy as jnp
from jax import lax
from jax.experimental import pallas as pl
from jax.experimental.pallas import tpu as pltpu
from jax.sharding import PartitionSpec as P

MESH = pl.DeviceIdType.MESH
F32 = jnp.float32
BF16 = jnp.bfloat16
MICRO = 4
ROWS = 32
NX = 4
PAD = 16
DOWN, UP, NEXT_DOWN, PREV_UP = ALL = (0, 1, 2, 3)
OWN, HOP = 0, 1
LAG = 2
CURVE = math.sqrt(2.0 / math.pi)


def by_rows(left, right):
    return lax.dot_general(left, right, (((1,), (1,)), ((), ())), preferred_element_type=F32)


def by_cols(left, right):
    return lax.dot_general(left, right, (((0,), (0,)), ((), ())), preferred_element_type=F32)


def times(left, right):
    return jnp.dot(left, right, preferred_element_type=F32)


def lane_mask(shift):
    row = lax.broadcasted_iota(jnp.int32, (ROWS, 128), 0)
    lane = lax.broadcasted_iota(jnp.int32, (ROWS, 128), 1)
    return lane == row + shift


def to_lanes(column, shift):
    return jnp.sum(jnp.where(lane_mask(shift), column, 0.0), 0, keepdims=True)


def to_column(lanes, shift):
    return jnp.sum(jnp.where(lane_mask(shift), lanes, 0.0), 1, keepdims=True)


def shard_rows(shards, unit, part):
    shape = (shards * unit, shards * PAD)
    row = lax.broadcasted_iota(jnp.int32, shape, 0)
    col = lax.broadcasted_iota(jnp.int32, shape, 1)
    hit = row < 0
    for k in range(shards):
        for i in range(unit if part is None else unit // 3):
            if part is None:
                hit |= (row == k * unit + i) & (col == k * PAD + i)
            else:
                hit |= (row == k * unit + 3 * i + part) & (col == k * PAD + unit + i)
    return jnp.where(hit, 1.0, 0.0).astype(BF16)


def relay_kernel(
    nz, copies, entry, exit_codes, exit_scale, slots, gain_ref, shard,
    sent, returned, grad_down, grad_up,
    zbuf, wv, span_src, span_in, spans, incf, incb, xs, norm_stat, pres, gsum,
    own_gain_down, next_gain_down, next_gain,
    p1s, p1r, t1s, t1r, p2s, p2r, t2s, t2r, u1s, u1r, u2s, u2r,
    gs, dxb, peak_src, peak_in, scaled, hidden, gb, dpre_s, pair_out, pair_in, own, zs, rz,
    span_sem, ssend, srecv, zsend, zrecv, xsend, xrecv, l1send, l1recv, l2send, l2recv,
    b1send, b1recv, b2send, b2recv, ysend, yrecv, wsend, wrecv, peak_sem,
    fsend, frecv, rsend, rrecv, psend, precv, gzsend, gzrecv,
):
    sec = lax.axis_index("section")
    last = lax.axis_size("section") - 1
    dp = lax.axis_index("dp")
    ten = lax.axis_index("tensor")
    x = dp // nz
    z = dp % nz
    half_z = nz // 2
    unit = grad_down.shape[0]
    cols = gain_ref.shape[1]
    half = cols // 2
    pack = shard.shape[2]
    bot = pres.shape[2]
    total = cols * 4
    xr, xl, xo = (x + 1) % NX, (x + NX - 1) % NX, (x + 2) % NX
    to_right = {"dp": xr * nz + z}
    to_left = {"dp": xl * nz + z}
    mate = {"tensor": ten + 1 - 2 * (ten % 2)}
    far = {"tensor": (ten + 2) % 4}
    others = [{"tensor": (ten + k) % 4} for k in (1, 2, 3)]
    next_sec = {"section": (sec + 1) % (last + 1)}
    prev_sec = {"section": (sec + last) % (last + 1)}
    z_up = {"dp": x * nz + (z + 1) % nz}
    z_down = {"dp": x * nz + (z + nz - 1) % nz}

    barrier = pltpu.get_barrier_semaphore()
    x_peers = [{"dp": (x + k) % NX * nz + z} for k in (1, 2, 3)]
    z_peers = [{"dp": x * nz + (z + 2 * k) % nz} for k in (1, 2, 3)]
    z_mate = {"dp": dp + 1 - 2 * (z % 2)}
    diagonal = [{"section": to["section"], "tensor": far["tensor"]} for to in (next_sec, prev_sec)]
    friends = others + [next_sec, prev_sec, z_up, z_down] + x_peers + z_peers + diagonal
    for friend in friends:
        pl.semaphore_signal(barrier, inc=1, device_id=friend, device_id_type=MESH)
    pl.semaphore_wait(barrier, len(friends))

    def move(src, dst, send, recv, device):
        return pltpu.make_async_remote_copy(
            src_ref=src, dst_ref=dst, send_sem=send, recv_sem=recv,
            device_id=device, device_id_type=MESH,
        )

    def each(step):
        def tick(m, carry):
            step(m)
            return carry

        lax.fori_loop(0, MICRO, tick, 0)

    has = {DOWN: None, UP: None, NEXT_DOWN: sec < last, PREV_UP: sec > 0}

    def if_has(m, step):
        if has[m] is None:
            step()
        else:
            pl.when(has[m])(step)

    def shard_move(m):
        if m == NEXT_DOWN:
            return move(shard.at[DOWN], zbuf.at[z, m], ssend.at[0], srecv.at[0], prev_sec)
        if m == PREV_UP:
            return move(shard.at[UP], zbuf.at[z, m], ssend.at[1], srecv.at[1], next_sec)
        return move(gain_ref, next_gain, ssend.at[2], srecv.at[2], prev_sec)

    def z_move(way, slot, m):
        return move(
            zbuf.at[slot, m], zbuf.at[slot, m], zsend.at[way, slot, m], zrecv.at[slot, m],
            z_up if way == 0 else z_down,
        )

    def z_begin(m):
        @pl.when(z < nz - 1)
        def _():
            z_move(0, z, m).start()

        @pl.when(z > 0)
        def _():
            z_move(1, z, m).start()

    def z_step(tick):
        for m in ALL:
            k = tick if m in (DOWN, UP) else tick - LAG

            def pass_on():
                @pl.when((k >= 1) & (z - k >= 0))
                def _():
                    z_move(0, z - k, m).wait_recv()

                    @pl.when(z < nz - 1)
                    def _():
                        z_move(0, z - k, m).start()

                @pl.when((k >= 1) & (z + k < nz))
                def _():
                    z_move(1, z + k, m).wait_recv()

                    @pl.when(z > 0)
                    def _():
                        z_move(1, z + k, m).start()

            if_has(m, pass_on)

    def z_steps(first, end):
        def step(k, carry):
            z_step(k)
            return carry

        lax.fori_loop(first, end, step, 0)

    group = [z // half_z, 1 - z // half_z]

    def x_move(p, m, kind):
        g = group[p]
        block, device, part = {
            0: (x, to_right, slice(None)),
            1: (x, to_left, slice(None)),
            2: (xl, to_right, slice(0, half)),
            3: (xr, to_left, slice(half, cols)),
        }[kind]
        ref = wv.at[m, block, g] if kind < 2 else wv.at[m, block, g, :, part]
        return move(ref, ref, xsend.at[p, m, kind], xrecv.at[p, m, kind], device)

    def x_arrival(p, m, kind):
        g = group[p]
        ref = {
            0: lambda: wv.at[m, xl, g],
            1: lambda: wv.at[m, xr, g],
            2: lambda: wv.at[m, xo, g, :, slice(0, half)],
            3: lambda: wv.at[m, xo, g, :, slice(half, cols)],
        }[kind]()
        move(ref, ref, xsend.at[p, m, kind], xrecv.at[p, m, kind], to_right).wait_recv()

    def x_own(p, m):
        g = group[p]
        block = zbuf[pl.ds(g * half_z, half_z), m].reshape(half_z * PAD, pack)
        wv[m, x, g, :, 0:pack] = times(shard_rows(half_z, unit, None), block).astype(BF16)
        tail = 0.0
        for j in range(3):
            tail += times(
                shard_rows(half_z, unit, j), block[:, j * (cols - pack) : (j + 1) * (cols - pack)]
            )
        wv[m, x, g, :, pack:cols] = tail.astype(BF16)
        x_move(p, m, 0).start()
        x_move(p, m, 1).start()

    def x_forward(p, m):
        x_arrival(p, m, 0)
        x_move(p, m, 2).start()
        x_arrival(p, m, 1)
        x_move(p, m, 3).start()

    def x_finish(m):
        for p in range(2):
            x_arrival(p, m, 2)
            x_arrival(p, m, 3)

    @pl.when(sec > 0)
    def _():
        shard_move(NEXT_DOWN).start()
        shard_move(None).start()

    @pl.when(sec < last)
    def _():
        shard_move(PREV_UP).start()

    for m in (DOWN, UP):
        zbuf[z, m] = shard[m]
        z_begin(m)

    def squares(m, carry):
        sums = []
        for k in range(2):
            rows = copies[k, slots[m]].astype(F32)
            sums.append(to_lanes(jnp.sum(rows * rows, 1, keepdims=True), m * ROWS))
        return carry[0] + sums[0], carry[1] + sums[1]

    nothing = jnp.zeros((1, 128), F32)
    square_in, square_out = lax.fori_loop(0, MICRO, squares, (nothing, nothing))
    span_src[...] = jnp.zeros((8, 128), F32)
    span_src[0:1] = square_in
    span_src[1:2] = square_out

    def span_move(k):
        return move(span_src, span_in.at[k], span_sem.at[0, k], span_sem.at[1, k], others[k])

    for k in range(3):
        span_move(k).start()

    @pl.when(sec < last)
    def _():
        shard_move(NEXT_DOWN).wait_recv()
        z_begin(NEXT_DOWN)

    @pl.when(sec > 0)
    def _():
        shard_move(PREV_UP).wait_recv()
        z_begin(PREV_UP)

    z_steps(1, half_z)
    x_own(0, DOWN)
    x_own(0, UP)
    z_steps(half_z, half_z + LAG)
    if_has(NEXT_DOWN, lambda: x_own(0, NEXT_DOWN))
    x_forward(0, DOWN)
    z_steps(half_z + LAG, half_z + LAG + 1)
    x_forward(0, UP)
    z_steps(half_z + LAG + 1, nz)
    x_own(1, DOWN)
    x_own(1, UP)
    if_has(NEXT_DOWN, lambda: x_forward(0, NEXT_DOWN))
    z_steps(nz, nz + LAG)
    for k in range(3):
        span_move(k).wait_recv()
    spans[...] = 2.0 * jnp.sqrt(
        (span_src[...] + span_in[0] + span_in[1] + span_in[2]) / total + 1e-05
    )
    x_forward(1, DOWN)
    if_has(NEXT_DOWN, lambda: x_own(1, NEXT_DOWN))
    x_forward(1, UP)
    x_finish(DOWN)
    for p in range(2):
        if_has(PREV_UP, lambda: x_own(p, PREV_UP))

    def weights(m):
        return wv[m].reshape(bot, cols)

    def gain_times(gain, m):
        first = gain.astype(BF16).astype(F32)
        second = (gain - first).astype(BF16).astype(F32)
        third = gain - first - second
        row = lax.broadcasted_iota(jnp.int32, (PAD, cols), 0)
        terms = jnp.where(
            row == 0, first, jnp.where(row == 1, second, jnp.where(row == 2, third, 0.0))
        ).astype(BF16)
        return jnp.sum(by_rows(terms, weights(m)), 0, keepdims=True)

    pieces = bot // 128

    def put_stat(ref, mean, spread, gd):
        ref[...] = jnp.zeros((8, 128), F32)
        ref[0:1] = to_lanes(mean, 0)
        ref[1:2] = to_lanes(spread, 0)
        for i in range(pieces):
            ref[2 + i : 3 + i] = gd[:, i * 128 : (i + 1) * 128]

    def get_stat(ref):
        gd = jnp.concatenate([ref[2 + i : 3 + i] for i in range(pieces)], axis=1)
        return to_column(ref[0:1], 0), to_column(ref[1:2], 0), gd

    def join(count, p, mean, spread, gd, p_other, mean_other, spread_other, gd_other):
        both = 0.5 * (mean + mean_other)
        mine, theirs = mean - both, mean_other - both
        spread_both = spread + spread_other + count * (mine * mine + theirs * theirs)
        p_both = (p + p_other) + (mine * gd + theirs * gd_other)
        return p_both, both, spread_both, gd + gd_other

    far_of, far_before = diagonal

    def l1(step, m):
        return [
            move(src.at[step, m], dst.at[step, m], l1send.at[step, m, i], l1recv.at[step, m, i], mate)
            for i, (src, dst) in enumerate(((p1s, p1r), (t1s, t1r)))
        ]

    def l2(step, m):
        places = [(1, far)] if step == OWN else [(0, next_sec), (1, far_of)]
        return [
            move(
                src.at[step, m], dst.at[place, m], l2send.at[step, m, i, place],
                l2recv.at[m, i, place], device,
            )
            for i, (src, dst) in enumerate(((p2s, p2r), (t2s, t2r)))
            for place, device in places
        ]

    def y_forward(m):
        return move(sent.at[m], incf.at[m], ysend.at[m], yrecv.at[m], next_sec)

    def y_back(m):
        return move(dxb.at[m], incb.at[m], wsend.at[m], wrecv.at[m], prev_sec)

    factors = (hidden, dpre_s)

    def factor_move(which, m, k):
        ref = factors[which].at[x, m]
        return move(ref, ref, fsend.at[which, m, k], frecv.at[which, m, k], x_peers[k])

    def factor_send(which, m):
        for k in range(3):
            factor_move(which, m, k).start()

    def factor_wait(which):
        def wait(m):
            for k in range(3):
                ref = factors[which].at[(x + NX - 1 - k) % NX, m]
                move(ref, ref, fsend.at[which, m, k], frecv.at[which, m, k], x_peers[k]).wait_recv()

        each(wait)

    ring_rows = (scaled, gb)

    def ring_move(which, m, kind):
        block, device, part = {
            0: (x, to_right, slice(None)),
            1: (x, to_left, slice(None)),
            2: (xl, to_right, slice(0, half)),
            3: (xr, to_left, slice(half, cols)),
        }[kind]
        rows = ring_rows[which]
        ref = rows.at[block, m] if kind < 2 else rows.at[block, m, :, part]
        return move(ref, ref, rsend.at[which, m, kind], rrecv.at[which, m, kind], device)

    def ring_arrival(which, m, kind):
        rows = ring_rows[which]
        ref = {
            0: lambda: rows.at[xl, m],
            1: lambda: rows.at[xr, m],
            2: lambda: rows.at[xo, m, :, slice(0, half)],
            3: lambda: rows.at[xo, m, :, slice(half, cols)],
        }[kind]()
        move(ref, ref, rsend.at[which, m, kind], rrecv.at[which, m, kind], to_right).wait_recv()

    def ring_send(which, m):
        ring_move(which, m, 0).start()
        ring_move(which, m, 1).start()

    def ring_forward(which):
        def step(m):
            ring_arrival(which, m, 0)
            ring_move(which, m, 2).start()
            ring_arrival(which, m, 1)
            ring_move(which, m, 3).start()

        each(step)

    def ring_end(which):
        def step(m):
            ring_arrival(which, m, 2)
            ring_arrival(which, m, 3)

        each(step)

    def enter_begin(step, m, rows, gain, gd, w):
        mean = jnp.sum(rows, 1, keepdims=True) / cols
        centred = rows - mean
        spread = jnp.sum(centred * centred, 1, keepdims=True)
        p1s[step, m] = by_rows((centred * gain).astype(BF16), weights(w))
        put_stat(t1s.at[step, m], mean, spread, gd)
        for copy in l1(step, m):
            copy.start()

    def enter_end(step, m):
        for copy in l1(step, m):
            copy.wait_recv()
        part, mean, spread, gd = join(
            float(cols), p1s[step, m], *get_stat(t1s.at[step, m]),
            p1r[step, m], *get_stat(t1r.at[step, m])
        )
        p2s[step, m] = part.astype(BF16)
        put_stat(t2s.at[step, m], mean, spread, gd)
        if step == OWN:
            p2r[0, m] = part.astype(BF16)
            put_stat(t2r.at[0, m], mean, spread, gd)
        for copy in l2(step, m):
            copy.start()

    def l2_arrival(place, m):
        for i, dst in enumerate((p2r, t2r)):
            move(
                dst.at[place, m], dst.at[place, m], l2send.at[HOP, m, i, place],
                l2recv.at[m, i, place], far,
            ).wait_recv()

    @pl.when(sec == 0)
    def _():
        own_gain_down[...] = gain_times(gain_ref[...], DOWN)

        def enter(m):
            span = to_column(spans[0:1], m * ROWS)
            rows = copies[0, slots[m]].astype(F32) + span * entry[m].astype(F32)
            xs[m] = rows
            enter_begin(OWN, m, rows, gain_ref[...], own_gain_down[...], DOWN)
            enter_end(OWN, m)

        each(enter)

    if_has(NEXT_DOWN, lambda: x_forward(1, NEXT_DOWN))
    x_finish(UP)

    @pl.when(sec > 0)
    def _():
        for p in range(2):
            x_forward(p, PREV_UP)

    @pl.when(sec < last)
    def _():
        x_finish(NEXT_DOWN)
        shard_move(None).wait_recv()
        next_gain_down[...] = gain_times(next_gain[...], NEXT_DOWN)

    def b1(step, m):
        return move(u1s.at[step, m], u1r.at[step, m], b1send.at[step, m], b1recv.at[step, m], mate)

    def b2(step, m):
        places = [(1, far)] if step == OWN else [(0, prev_sec), (1, far_before)]
        return [
            move(
                u2s.at[step, m], u2r.at[place, m], b2send.at[step, m, place],
                b2recv.at[m, place], device,
            )
            for place, device in places
        ]

    def b2_arrival(place, m):
        move(
            u2r.at[place, m], u2r.at[place, m], b2send.at[HOP, m, place],
            b2recv.at[m, place], far,
        ).wait_recv()

    def back_begin(step, m, rows, w):
        u1s[step, m] = by_rows(rows, weights(w))
        b1(step, m).start()

    def back_end(step, m):
        b1(step, m).wait_recv()
        both = (u1s[step, m] + u1r[step, m]).astype(BF16)
        u2s[step, m] = both
        if step == OWN:
            u2r[0, m] = both
        for copy in b2(step, m):
            copy.start()

    def backward(m):
        b2_arrival(1, m)
        grad_act = u2r[0, m].astype(F32) + u2r[1, m].astype(F32)
        pre = pres[m]
        bend = jnp.tanh(CURVE * (pre + 0.044715 * (pre * pre * pre)))
        slope = 0.5 * (1.0 + bend) + 0.5 * pre * (1.0 - bend * bend) * (
            CURVE * (1.0 + 3.0 * 0.044715 * pre * pre)
        )
        dpre = (grad_act * slope).astype(BF16)
        dpre_s[x, m] = dpre
        factor_send(1, m)
        wide = dpre.astype(F32)
        mean_grad = jnp.sum(wide * gsum[...], 1, keepdims=True) / total
        mean_cross = jnp.sum(wide * pre, 1, keepdims=True) / total
        mean, inverse = norm_stat[m, 0], norm_stat[m, 1]
        normed = (xs[m] - mean) * inverse
        dn = times(dpre, weights(DOWN)) * gain_ref[...]
        dx = gs[m] + inverse * (dn - mean_grad - normed * mean_cross)
        gs[m] = dx
        dxb[m] = dx.astype(BF16)

        @pl.when(sec > 0)
        def _():
            y_back(m).start()
            back_begin(HOP, m, dxb[m], PREV_UP)

        peak_src[0:1] += to_lanes(jnp.max(jnp.abs(dx), 1, keepdims=True), m * ROWS)

        @pl.when(sec > 0)
        def _():
            back_end(HOP, m)

    peak_src[...] = jnp.zeros((8, 128), F32)

    @pl.when(sec == last)
    def _():
        def enter(m):
            gs[m] = exit_codes[m].astype(F32) * exit_scale[m]
            gb[x, m] = gs[m].astype(BF16)
            back_begin(OWN, m, gb[x, m], UP)
            ring_send(1, m)
            back_end(OWN, m)

        each(enter)
        x_finish(PREV_UP)

    def forward(m):
        @pl.when(sec > 0)
        def _():
            y_forward(m).wait_recv()
            span = to_column(spans[0:1], m * ROWS)
            xs[m] = copies[0, slots[m]].astype(F32) + span * incf[m].astype(F32)
            l2_arrival(0, m)

        l2_arrival(1, m)
        raw, mean, spread, gd = join(
            float(2 * cols), p2r[0, m].astype(F32), *get_stat(t2r.at[0, m]),
            p2r[1, m].astype(F32), *get_stat(t2r.at[1, m])
        )
        inverse = lax.rsqrt(spread / total + 1e-05)
        pre = raw * inverse
        gsum[...] = gd
        pres[m] = pre
        norm_stat[m, 0] = mean
        norm_stat[m, 1] = inverse
        act = (0.5 * pre * (1.0 + jnp.tanh(CURVE * (pre + 0.044715 * (pre * pre * pre))))).astype(BF16)
        hidden[x, m] = act
        result = xs[m] + times(act, weights(UP))
        span = to_column(spans[1:2], m * ROWS)
        copy_out = copies[1, slots[m]].astype(F32)
        codes = jnp.clip((result - copy_out) / span, -1.0, 1.0).astype(BF16)
        sent[m] = codes

        @pl.when(sec < last)
        def _():
            y_forward(m).start()
            rows = copy_out + span * codes.astype(F32)
            enter_begin(HOP, m, rows, next_gain[...], next_gain_down[...], NEXT_DOWN)

        scaled[x, m] = ((xs[m] - mean) * inverse * gain_ref[...]).astype(BF16)
        ring_send(0, m)
        factor_send(0, m)

        @pl.when(sec < last)
        def _():
            enter_end(HOP, m)

        @pl.when(sec == last)
        def _():
            backward(m)

    each(forward)
    ring_forward(0)

    @pl.when(sec < last)
    def _():
        @pl.when(sec > 0)
        def _():
            x_finish(PREV_UP)

        def back(m):
            y_back(m).wait_recv()
            gs[m] = incb[m].astype(F32)
            gb[x, m] = incb[m]
            ring_send(1, m)
            b2_arrival(0, m)
            backward(m)

        each(back)

    ring_forward(1)

    quarter = nz // 2
    parity = z % 2

    def unit_pick(side):
        shape = (bot, quarter * unit)
        row = lax.broadcasted_iota(jnp.int32, shape, 0)
        col = lax.broadcasted_iota(jnp.int32, shape, 1)
        source = col + (x * nz + side) * unit
        for k in range(1, quarter):
            source += jnp.where(col >= k * unit, unit, 0)
        return jnp.where(row == source, 1.0, 0.0).astype(BF16)

    def gradient(p, side):
        left, right = (hidden, gb) if p < 2 else (dpre_s, scaled)
        tokens = NX * MICRO * ROWS
        at = slice(p % 2 * half, (p % 2 + 1) * half)
        lhs = times(left[...].reshape(tokens, bot), unit_pick(side)).astype(BF16)
        return by_cols(lhs, right[:, :, :, at].reshape(tokens, half))

    def pair_move(p):
        return move(pair_out.at[p], pair_in.at[p], psend.at[p], precv.at[p], z_mate)

    def gz_move(k):
        slot = (z + 2 * (k + 1)) % nz // 2
        return move(zs.at[slot], rz.at[k], gzsend.at[k], gzrecv.at[k], z_peers[k])

    def piece_rows(p):
        shape = (quarter * 4 * unit, quarter * unit)
        row = lax.broadcasted_iota(jnp.int32, shape, 0)
        col = lax.broadcasted_iota(jnp.int32, shape, 1)
        target = col + p * unit
        for k in range(1, quarter):
            target += jnp.where(col >= k * unit, 3 * unit, 0)
        return jnp.where(row == target, 1.0, 0.0).astype(BF16)

    def gradient_first(pieces):
        for p in pieces:
            pair_out[p] = gradient(p, 1 - parity).astype(BF16)
            pair_move(p).start()

    def gradient_own():
        for p in range(4):
            own[p] = gradient(p, parity)

    def gradient_second():
        rows = 0.0
        for p in (2, 3, 0, 1):
            pair_move(p).wait_recv()
            both = (own[p] + pair_in[p].astype(F32)).astype(BF16)
            rows += times(piece_rows(p), both)
        zs[...] = rows.astype(BF16).reshape(quarter, 4 * unit, half)
        for k in range(3):
            gz_move(k).start()

    def peak_move(k):
        return move(peak_src, peak_in.at[k], peak_sem.at[0, k], peak_sem.at[1, k], others[k])

    for k in range(3):
        peak_move(k).start()
    ring_end(0)
    factor_wait(1)
    gradient_first((2, 3))
    factor_wait(0)
    ring_end(1)
    gradient_first((0, 1))
    gradient_own()
    gradient_second()

    for k in range(3):
        peak_move(k).wait_recv()
    peak_row = jnp.maximum(
        jnp.maximum(peak_src[0:1], peak_in[0, 0:1]),
        jnp.maximum(peak_in[1, 0:1], peak_in[2, 0:1]),
    )
    peak_row = (peak_row + 1e-05).astype(BF16).astype(F32)

    def codes_back(m):
        returned[m] = (gs[m] / to_column(peak_row, m * ROWS)).astype(BF16)

    each(codes_back)

    result = zs[z // 2].astype(F32)
    for k in range(3):
        gz_move(k).wait_recv()
        result += rz[k].astype(F32)
    own[0] = result
    for p in range(4):
        out = grad_up if p < 2 else grad_down
        out[:, p % 2 * half : (p % 2 + 1) * half] = own[0, p * unit : (p + 1) * unit]

    for k in range(3):
        span_move(k).wait_send()
        peak_move(k).wait_send()

    def drain_micro(m):
        @pl.when(sec == 0)
        def _():
            for copy in l1(OWN, m) + l2(OWN, m):
                copy.wait_send()

        @pl.when(sec == last)
        def _():
            for copy in [b1(OWN, m)] + b2(OWN, m):
                copy.wait_send()

        @pl.when(sec < last)
        def _():
            for copy in l1(HOP, m) + l2(HOP, m) + [y_forward(m)]:
                copy.wait_send()

        @pl.when(sec > 0)
        def _():
            for copy in [b1(HOP, m)] + b2(HOP, m) + [y_back(m)]:
                copy.wait_send()

    each(drain_micro)

    @pl.when(sec > 0)
    def _():
        shard_move(NEXT_DOWN).wait_send()
        shard_move(None).wait_send()

    @pl.when(sec < last)
    def _():
        shard_move(PREV_UP).wait_send()

    for m in ALL:
        def drain_x():
            for p in range(2):
                for kind in range(4):
                    x_move(p, m, kind).wait_send()

        if_has(m, drain_x)

    for p in range(4):
        pair_move(p).wait_send()
    for k in range(3):
        gz_move(k).wait_send()

    def drain_factors(m):
        for which in range(2):
            for k in range(3):
                factor_move(which, m, k).wait_send()
        for which in range(2):
            for kind in range(4):
                ring_move(which, m, kind).wait_send()

    each(drain_factors)

    def drain_z(slot, carry):
        for m in ALL:
            def drain():
                @pl.when((z < nz - 1) & (slot <= z))
                def _():
                    z_move(0, slot, m).wait_send()

                @pl.when((z > 0) & (slot >= z))
                def _():
                    z_move(1, slot, m).wait_send()

            if_has(m, drain)

        return carry

    lax.fori_loop(0, nz, drain_z, 0)


def solution(mesh):
    nz = mesh.shape["dp"] // NX

    def local(stored, entry, exit_codes, exit_scales, slot_ids, gain, down, up):
        unit, cols = down.shape[1], down.shape[2]
        bot = unit * mesh.shape["dp"]
        tokens = MICRO * ROWS
        pack = cols * unit // PAD // 128 * 128 + 128

        def packed(w):
            tail = w[:, pack:].reshape(PAD - unit, unit // (PAD - unit) * (cols - pack))
            tail = jnp.pad(tail, ((0, 0), (0, pack - tail.shape[1])))
            return jnp.concatenate([w[:, :pack], tail])

        shard = jnp.stack([packed(down[0]), packed(up[0])])
        block = (MICRO, ROWS, cols)
        small = (MICRO, ROWS, bot)
        stat = (2, MICRO, 8, 128)
        dma = pltpu.SemaphoreType.DMA
        vm = pltpu.VMEM
        xrows = bot // NX
        scratch = [
            vm((nz, 4, PAD, pack), BF16),
            vm((4, NX, 2, xrows // 2, cols), BF16),
            vm((8, 128), F32), vm((3, 8, 128), F32), vm((8, 128), F32),
            vm(block, BF16), vm(block, BF16),
            vm(block, F32),
            vm((MICRO, 2, ROWS, 1), F32),
            vm(small, F32),
            vm((1, bot), F32), vm((1, bot), F32), vm((1, bot), F32), vm((1, cols), F32),
            vm((2, *small), F32), vm((2, *small), F32), vm(stat, F32), vm(stat, F32),
            vm((2, *small), BF16), vm((2, *small), BF16), vm(stat, F32), vm(stat, F32),
            vm((2, *small), F32), vm((2, *small), F32),
            vm((2, *small), BF16), vm((2, *small), BF16),
            vm(block, F32), vm(block, BF16),
            vm((8, 128), F32), vm((3, 8, 128), F32),
            vm((NX, *block), BF16), vm((NX, *small), BF16),
            vm((NX, *block), BF16), vm((NX, *small), BF16),
            vm((4, xrows // 2, cols // 2), BF16), vm((4, xrows // 2, cols // 2), BF16),
            vm((4, xrows // 2, cols // 2), F32),
            vm((nz // 2, 4 * unit, cols // 2), BF16),
            vm((3, 4 * unit, cols // 2), BF16),
            dma((2, 3)),
            dma((3,)), dma((3,)),
            dma((2, nz, 4)), dma((nz, 4)),
            dma((2, 4, 4)), dma((2, 4, 4)),
            dma((2, MICRO, 2)), dma((2, MICRO, 2)), dma((2, MICRO, 2, 2)), dma((MICRO, 2, 2)),
            dma((2, MICRO)), dma((2, MICRO)), dma((2, MICRO, 2)), dma((MICRO, 2)),
            dma((MICRO,)), dma((MICRO,)), dma((MICRO,)), dma((MICRO,)),
            dma((2, 3)),
            dma((2, MICRO, 3)), dma((2, MICRO, 3)),
            dma((2, MICRO, 4)), dma((2, MICRO, 4)),
            dma((4,)), dma((4,)),
            dma((3,)), dma((3,)),
        ]
        in_vmem = pl.BlockSpec(memory_space=pltpu.VMEM)
        sent, returned, grad_down, grad_up = pl.pallas_call(
            lambda *refs: relay_kernel(nz, *refs),
            out_shape=(
                jax.ShapeDtypeStruct(block, BF16),
                jax.ShapeDtypeStruct(block, BF16),
                jax.ShapeDtypeStruct((unit, cols), F32),
                jax.ShapeDtypeStruct((unit, cols), F32),
            ),
            in_specs=[in_vmem] * 4 + [pl.BlockSpec(memory_space=pltpu.SMEM)] + [in_vmem] * 2,
            out_specs=(in_vmem,) * 4,
            scratch_shapes=scratch,
            compiler_params=pltpu.CompilerParams(
                collective_id=0, has_side_effects=True, vmem_limit_bytes=48 * 2**20
            ),
        )(
            stored[0].reshape(2, MICRO, ROWS, cols),
            entry.reshape(block),
            exit_codes.reshape(block),
            exit_scales.reshape(MICRO, ROWS, 1),
            slot_ids[0],
            gain,
            shard,
        )
        return (
            sent.reshape(1, tokens, cols),
            returned.reshape(1, tokens, cols),
            grad_down[None],
            grad_up[None],
        )

    in_specs = (
        P("section", None, "dp", "tensor"),
        P("dp", "tensor"),
        P("dp", "tensor"),
        P("dp"),
        P("dp", None),
        P("section", "tensor"),
        P("section", "dp", "tensor"),
        P("section", "dp", "tensor"),
    )
    out_specs = (P("section", "dp", "tensor"),) * 4
    return jax.shard_map(local, mesh=mesh, in_specs=in_specs, out_specs=out_specs, check_vma=False)
```
